32 devices in a mesh: lat: 4 (over y, x), lon: 8 (over z, core).
Axes of the slice: x: 2, y: 2, z: 4, core: 2. Of those that a mesh axis runs over, the one named last changes fastest.
Arguments:
- latent_state: bfloat16 [2, 96, 192, 1024], P(None, 'lat', 'lon'), may hold values from -6 to 6
- obs_rows: bfloat16 [4, 8, 1024, 256], P('lat', 'lon'), may hold values from -6 to 6
- obs_cells: int32 [4, 8, 1024], P('lat', 'lon'), may hold values from 0 to 1151
- obs_counts: int32 [4, 8, 32], P('lat', 'lon'), may hold values from 0 to 32, as said below
- w_obs: bfloat16 [256, 1024], replicated, may hold values from -0.375 to 0.375
- w_qkv: bfloat16 [1024, 3072], replicated, may hold values from -0.1875 to 0.1875
- w_out: bfloat16 [1024, 1024], replicated, may hold values from -0.1875 to 0.1875
- logit_scale: float32 [16], replicated, may hold values from 3 to 24
- pos_bias: float32 [16, 144, 144], replicated, may hold values from -4 to 4
- out_gain: float32 [1024], replicated, may hold values from 0.25 to 1.75
Outputs:
- shifted: bfloat16 [2, 96, 192, 1024], P(None, 'lat', 'lon')
The draws below stay inside these ranges and needn't reach their ends.
Inputs may be any that keep to these rules, and one draw needn't show every extreme that they name: `obs_counts`: at most 32 live slots from one source for one destination; in every draw some destination gets 32 live slots from every source. `obs_cells`: cells of a device are numbered level, latitude, longitude.
All inputs are finite; a program needn't handle non-finite values.
Results may differ from the reference program's by a relative error of at most 0.0066.
Values may be sent and summed in bfloat16 or wider, within the bound.
No kernel may reach another device: no remote copies, remote signals or barrier semaphores. Data moves between devices by JAX's collectives and lax.ppermute only.
A program may use at most 192 MiB of HBM per device.

```python
import math
import jax
import jax.numpy as jnp
from jax import lax

D = 1024
HEADS = 16
OBS_CH = 256
WL = 2
WA = 12
WO = 6
LEV = 2
CAP = 32
WTOK = 144
CLAT = 24
CLON = 24
TOK_DEV = 1152
NLAT = 96
NLON = 192
SLOTS = 1024
N_LAT = 4
N_LON = 8
DEVICES = 32


def draw_obs_counts(key, part):
    key = jax.random.fold_in(key, 7)
    key_level, key_raw, key_full = jax.random.split(key, 3)
    density = jax.random.randint(key_level, (DEVICES,), 1, 4)
    raw_draw = jax.random.randint(key_raw, (DEVICES, DEVICES), 0, 1 << 20)
    floor_count = density[None, :] * CAP // 6
    counts = floor_count + raw_draw % (density[None, :] * CAP // 3 + 1)
    counts = jnp.minimum(counts, CAP)
    full_dest = jax.random.randint(key_full, (), 0, DEVICES)
    column_ids = jnp.arange(DEVICES)[None, :]
    counts = jnp.where(column_ids == full_dest, CAP, counts)
    return counts.reshape(N_LAT, N_LON, DEVICES).astype(jnp.int32)


def plant(entries, own_key, smallest, largest):
    dims = entries.shape
    spot = [jax.random.randint(jax.random.fold_in(own_key, axis), (), 0, dims[axis]) for axis in range(len(dims))]
    entries = entries.at[tuple(spot)].set(smallest)
    longest = dims.index(max(dims))
    spot[longest] = (spot[longest] + 1) % dims[longest]
    return entries.at[tuple(spot)].set(largest)


def levels(own_key, shape, pieces, low, top_value):
    gain, own = 1.0, jax.random.fold_in(own_key, 6)
    for axis_at, shards_of in pieces:
        steps = jnp.exp(jax.random.uniform(jax.random.fold_in(own, axis_at), (shards_of,), jnp.float32, low / len(pieces), top_value / len(pieces)))
        gain = gain * jnp.repeat(steps, shape[axis_at] // shards_of).reshape([-1 if axis == axis_at else 1 for axis in range(len(shape))])
    return gain


def noise(rng, dims, scale, most, cuts=(), kind=jnp.bfloat16):
    array = scale * jax.random.normal(rng, dims, jnp.float32)
    if cuts:
        array = array * levels(rng, dims, cuts, -0.22, 0.18)
    return jnp.clip(array, -most, most).astype(kind)


def setup_inputs(seed: int = 0) -> dict:
    seeds = jax.random.split(jax.random.key(seed), 11)
    latent_state = noise(seeds[0], (LEV, NLAT, NLON, D), 1.0, 6.0, ((1, 4), (2, 8)))
    obs_rows = noise(seeds[1], (N_LAT, N_LON, SLOTS, OBS_CH), 1.0, 6.0, ((0, 4), (1, 8)))
    obs_cells = plant(jax.random.randint(seeds[2], (N_LAT, N_LON, SLOTS), 0, TOK_DEV), jax.random.fold_in(seeds[2], 1), 0, TOK_DEV - 1).astype(jnp.int32)
    obs_counts = draw_obs_counts(jax.random.fold_in(seeds[10], 71), 0)
    w_obs = noise(seeds[4], (OBS_CH, D), OBS_CH ** -0.5, 0.375)
    w_qkv = noise(seeds[5], (D, 3 * D), D ** -0.5, 0.1875)
    w_out = noise(seeds[6], (D, D), D ** -0.5, 0.1875)
    logit_scale = jnp.clip(jnp.exp(jax.random.uniform(seeds[7], (HEADS,), jnp.float32, math.log(3.0), math.log(24.0))), 3.0, 24.0)
    pos_bias = noise(seeds[8], (HEADS, WTOK, WTOK), 1.0, 4.0, (), jnp.float32)
    out_gain = jnp.clip(1.0 + 0.15 * jax.random.normal(seeds[9], (D,), jnp.float32), 0.25, 1.75)
    return dict(latent_state=latent_state, obs_rows=obs_rows, obs_cells=obs_cells, obs_counts=obs_counts, w_obs=w_obs, w_qkv=w_qkv, w_out=w_out, logit_scale=logit_scale, pos_bias=pos_bias, out_gain=out_gain)


cosine_eps = 1e-06
layer_eps = 1e-05

def attend_windows(windows, w_qkv, w_out, logit_scale, pos_bias, out_gain):
    count = windows.shape[0]
    flat = windows.reshape(count * WTOK, D)
    packed = jnp.dot(flat.astype(jnp.bfloat16), w_qkv, preferred_element_type=jnp.float32)
    packed = packed.reshape(count, WTOK, 3, HEADS, D // HEADS)
    query = packed[:, :, 0]
    keys = packed[:, :, 1]
    values = packed[:, :, 2].astype(jnp.bfloat16)
    query_n = (query * lax.rsqrt(lax.optimization_barrier(jnp.sum(query * query, -1, keepdims=True)) + cosine_eps)).astype(jnp.bfloat16)
    keys_n = (keys * lax.rsqrt(lax.optimization_barrier(jnp.sum(keys * keys, -1, keepdims=True)) + cosine_eps)).astype(jnp.bfloat16)
    scores = jnp.einsum('nqhd,nkhd->nhqk', query_n.astype(jnp.float32), keys_n.astype(jnp.float32))
    scores = scores * logit_scale[None, :, None, None] + pos_bias[None]
    expo = jnp.exp(scores)
    probs = (expo / lax.optimization_barrier(jnp.sum(expo, -1, keepdims=True))).astype(jnp.bfloat16)
    context = jnp.einsum('nhqk,nkhd->nqhd', probs.astype(jnp.float32), values.astype(jnp.float32))
    context = context.astype(jnp.bfloat16).reshape(count * WTOK, D)
    proj = jnp.dot(context, w_out, preferred_element_type=jnp.float32)
    center = proj - lax.optimization_barrier(jnp.mean(proj, -1, keepdims=True))
    spread = lax.optimization_barrier(jnp.mean(center * center, -1, keepdims=True))
    normed = center * lax.rsqrt(spread + layer_eps) * out_gain[None, :]
    return (flat + normed).astype(jnp.bfloat16).reshape(count, WTOK, D)

def reference(latent_state, obs_rows, obs_cells, obs_counts, w_obs, w_qkv, w_out, logit_scale, pos_bias, out_gain):
    total_cells = LEV * NLAT * NLON
    slot_ids = jnp.arange(SLOTS).astype(jnp.int32)
    target = slot_ids // CAP
    target_lat = target // N_LON
    target_lon = target % N_LON
    slot_in = slot_ids % CAP
    rows_all = obs_rows.reshape(DEVICES, SLOTS, OBS_CH)
    cells_all = obs_cells.reshape(DEVICES, SLOTS).astype(jnp.int32)
    counts_all = obs_counts.reshape(DEVICES, DEVICES).astype(jnp.int32)
    level_of = cells_all // (CLAT * CLON)
    lat_of = cells_all // CLON % CLAT
    lon_of = cells_all % CLON
    global_index = ((level_of * NLAT + target_lat[None, :] * CLAT + lat_of) * NLON + target_lon[None, :] * CLON + lon_of).astype(jnp.int32)
    live = (slot_in[None, :] < counts_all[:, target]).astype(jnp.float32)

    def add_source(source, total):
        encoded = jnp.dot(rows_all[source], w_obs, preferred_element_type=jnp.float32) * live[source][:, None]
        return total.at[global_index[source]].add(encoded)
    start = latent_state.reshape(total_cells, D).astype(jnp.float32)
    latent = lax.fori_loop(0, DEVICES, add_source, start)
    grid = latent.reshape(LEV // WL, WL, NLAT // WA, WA, NLON // WO, WO, D)
    blocks = grid.transpose(2, 0, 4, 1, 3, 5, 6).reshape(NLAT // WA, LEV // WL * (NLON // WO), WTOK, D)

    def one_band(band):
        return attend_windows(band, w_qkv, w_out, logit_scale, pos_bias, out_gain)
    done = lax.map(one_band, blocks)
    done = done.reshape(NLAT // WA, LEV // WL, NLON // WO, WL, WA, WO, D).transpose(1, 3, 0, 4, 2, 5, 6)
    updated = done.reshape(LEV, NLAT, NLON, D)
    moved = jnp.roll(updated, WL // 2, axis=0)
    moved = jnp.roll(moved, WO // 2, axis=2)
    filler = jnp.zeros((LEV, WA // 2, NLON, D), jnp.bfloat16)
    return jnp.concatenate([filler, moved[:, :NLAT - WA // 2]], axis=1)
```

```python
import functools
import math

import jax
import jax.numpy as jnp
from jax import lax
from jax.experimental import pallas as pl
from jax.experimental.pallas import tpu as pltpu
from jax.sharding import PartitionSpec as P

WL = 2
WA = 12
WO = 6
CELLS = WL * WA * WO
HALF_A = WA // 2
HALF_O = WO // 2
GROUP = 256
EDGE = 48

cosine_eps = 1e-06
layer_eps = 1e-05
LOG2E = math.log2(math.e)

F32 = jnp.float32
BF16 = jnp.bfloat16


def divided(x, n):
    quotient = lax.div(x, jnp.full_like(x, n))
    return quotient, x - quotient * n


def window_parts(row):
    window, inner = divided(row, CELLS)
    level, inner = divided(inner, WA * WO)
    lat, lon = divided(inner, WO)
    return window, level, lat, lon


def dot(a, b):
    return jnp.dot(a, b, preferred_element_type=F32)


def project_kernel(lon_cells, latent_ref, w_obs_ref, w_ref, base_ref, folded_ref, ordered_ref, left):
    rows = latent_ref.shape[0]
    strip = WL * WA * lon_cells
    strips = rows // strip
    part = WA * lon_cells

    @pl.when(pl.program_id(0) == 0)
    def _():
        row = lax.broadcasted_iota(jnp.int32, (strip, 1), 0)
        window, level, lat, lon = window_parts(row)
        source = level * part + lat * lon_cells + window * WO + lon
        perm = (source == lax.broadcasted_iota(jnp.int32, (1, strip), 1)).astype(F32).astype(BF16)
        for s in range(strips):
            cells = jnp.concatenate(
                [
                    latent_ref[l * strips * part + s * part : l * strips * part + (s + 1) * part]
                    for l in range(WL)
                ],
                axis=0,
            )
            moved = dot(perm, cells).astype(BF16)
            left[s * strip : (s + 1) * strip] = moved
            ordered_ref[s * strip : (s + 1) * strip] = moved
        left[rows:] = w_obs_ref[...]

    result = dot(left[...], w_ref[...])
    base_ref[...] = result[:rows]
    folded_ref[...] = result[rows:].astype(BF16)


def project(latent, w_obs, w_qkv, lon_cells):
    rows, features = latent.shape
    channels = w_obs.shape[0]
    columns = w_qkv.shape[1]
    whole = lambda i: (0, 0)
    block = lambda i: (0, i)
    return pl.pallas_call(
        functools.partial(project_kernel, lon_cells),
        grid=(columns // GROUP,),
        in_specs=[
            pl.BlockSpec((rows, features), whole),
            pl.BlockSpec((channels, features), whole),
            pl.BlockSpec((features, GROUP), block),
        ],
        out_specs=[
            pl.BlockSpec((rows, GROUP), block),
            pl.BlockSpec((channels, GROUP), block),
            pl.BlockSpec((rows, features), whole),
        ],
        out_shape=[
            jax.ShapeDtypeStruct((rows, columns), F32),
            jax.ShapeDtypeStruct((channels, columns), BF16),
            jax.ShapeDtypeStruct((rows, features), BF16),
        ],
        scratch_shapes=[pltpu.VMEM((rows + channels, features), BF16)],
        compiler_params=pltpu.CompilerParams(vmem_limit_bytes=40 * 1024 * 1024),
        cost_estimate=pl.CostEstimate(
            flops=2 * (rows + channels) * features * columns,
            bytes_accessed=4 * rows * columns + 2 * features * columns + 4 * rows * features,
            transcendentals=0,
        ),
    )(latent, w_obs, w_qkv)


def strip_kernel(
    strip_at,
    lon_cells,
    lat_cells,
    targets_ref,
    rows_ref,
    base_q_ref,
    base_k_ref,
    base_v_ref,
    fold_q_ref,
    fold_k_ref,
    fold_v_ref,
    ordered_ref,
    w_obs_ref,
    w_out_ref,
    scale_ref,
    bias_ref,
    gain_ref,
    near_ref,
    far_ref,
    near_edge_ref,
    far_edge_ref,
    gathered,
    context,
    finished,
):
    step = pl.program_id(0)
    strip = ordered_ref.shape[0]
    features = ordered_ref.shape[1]
    windows = strip // CELLS
    slots = targets_ref.shape[1]
    chunk = 1024
    heads = bias_ref.shape[0]
    head_width = GROUP // heads

    @pl.when(step == 0)
    def _():
        row = lax.broadcasted_iota(jnp.int32, (strip, 1), 0)
        window, level, lat, lon = window_parts(row)
        cell = (level * lat_cells + strip_at * WA + lat) * lon_cells + window * WO + lon
        total = jnp.zeros((strip, rows_ref.shape[1]), F32)
        for at in range(0, slots, chunk):
            hits = (cell == targets_ref[:, at : at + chunk]).astype(F32).astype(BF16)
            total += dot(hits, rows_ref[at : at + chunk])
        high = total.astype(BF16)
        gathered[:, : GROUP] = high
        gathered[:, GROUP:] = (total - high.astype(F32)).astype(BF16)

    lane_head = lax.broadcasted_iota(jnp.int32, (1, GROUP), 1) // head_width
    same_head = (
        (lax.broadcasted_iota(jnp.int32, (GROUP, 1), 0) // head_width == lane_head)
        .astype(F32)
        .astype(BF16)
    )
    masks = [(lane_head == h).astype(F32).astype(BF16) for h in range(heads)]
    ones_bd = jnp.concatenate(
        [jnp.broadcast_to(masks[h], (CELLS, GROUP)) for h in range(heads)], axis=0
    )
    bias = jnp.concatenate([bias_ref[h] for h in range(heads)], axis=1) * LOG2E

    high = gathered[:, :GROUP]
    query = base_q_ref[...] + dot(high, fold_q_ref[...])
    keys = base_k_ref[...] + dot(high, fold_k_ref[...])
    values = (base_v_ref[...] + dot(high, fold_v_ref[...])).astype(BF16)
    query_sum = dot((query * query).astype(BF16), same_head)
    keys_sum = dot((keys * keys).astype(BF16), same_head)
    query_n = (query * (lax.rsqrt(query_sum + cosine_eps) * scale_ref[...])).astype(BF16)
    keys_n = (keys * lax.rsqrt(keys_sum + cosine_eps)).astype(BF16)
    parts = []
    for w in range(windows):
        here = slice(w * CELLS, (w + 1) * CELLS)
        keys_w = keys_n[here]
        values_w = values[here]
        keys_bd = jnp.concatenate([keys_w * masks[h] for h in range(heads)], axis=0)
        values_bd = jnp.concatenate([values_w * masks[h] for h in range(heads)], axis=0)
        scores = lax.dot_general(
            query_n[here], keys_bd, (((1,), (1,)), ((), ())), preferred_element_type=F32
        )
        expo = jnp.exp2(scores + bias).astype(BF16)
        weighted = dot(expo, values_bd)
        norm = dot(expo, ones_bd)
        context[step, here] = (weighted / norm).astype(BF16)

    @pl.when(step == pl.num_programs(0) - 1)
    def _():
        w_obs = w_obs_ref[...]
        w_obs_twice = jnp.concatenate([w_obs, w_obs], axis=0)
        pieces = 2
        size = strip // pieces
        for at in range(pieces):
            here = slice(at * size, (at + 1) * size)
            proj = jnp.zeros((size, features), F32)
            for g in range(features // GROUP):
                proj += dot(context[g, here], w_out_ref[g * GROUP : (g + 1) * GROUP])
            latent = ordered_ref[here].astype(F32) + dot(gathered[here], w_obs_twice)
            center = proj - jnp.mean(proj, -1, keepdims=True)
            spread = jnp.mean(center * center, -1, keepdims=True)
            normed = center * lax.rsqrt(spread + layer_eps) * gain_ref[...]
            finished[here] = (latent + normed).astype(BF16)
        row = lax.broadcasted_iota(jnp.int32, (1, strip), 1)
        window, level, lat, lon = window_parts(row)
        level = lax.rem(level + WL // 2, jnp.full_like(level, WL))
        half, lat = divided(lat, HALF_A)
        lon = window * WO + lon
        moved = lax.rem(lon + HALF_O, jnp.full_like(lon, lon_cells))
        place = ((half * WL + level) * HALF_A + lat) * lon_cells + moved
        edge = (level * HALF_A + lat) * HALF_O + moved
        in_edge = moved < HALF_O
        done = finished[...]
        size = WL * HALF_A * lon_cells
        for h, (out_ref, edge_ref) in enumerate(
            ((near_ref, near_edge_ref), (far_ref, far_edge_ref))
        ):
            index = lax.broadcasted_iota(jnp.int32, (size, 1), 0) + h * size
            out_ref[...] = dot((index == place).astype(F32).astype(BF16), done).astype(BF16)
            index = lax.broadcasted_iota(jnp.int32, (EDGE, 1), 0)
            index = jnp.where(in_edge & (half == h), edge, -1) == index
            edge_ref[...] = dot(index.astype(F32).astype(BF16), done).astype(BF16)


def attend_strip(
    strip_at, targets, rows, base, folded, ordered, w_obs, w_out, scale, bias, gain, lat_cells, lon_cells
):
    strip = WL * WA * lon_cells
    features = w_out.shape[0]
    groups = features // GROUP
    channels = w_obs.shape[0]
    heads = bias.shape[0] // groups
    size = strip // 2
    whole = lambda i: (0, 0)
    once = pl.Buffered(buffer_count=1)
    return pl.pallas_call(
        functools.partial(strip_kernel, strip_at, lon_cells, lat_cells),
        grid=(groups,),
        in_specs=[
            pl.BlockSpec(targets.shape, whole, pipeline_mode=once),
            pl.BlockSpec(rows.shape, whole, pipeline_mode=once),
            pl.BlockSpec((strip, GROUP), lambda i: (strip_at, i)),
            pl.BlockSpec((strip, GROUP), lambda i: (strip_at, groups + i)),
            pl.BlockSpec((strip, GROUP), lambda i: (strip_at, 2 * groups + i)),
            pl.BlockSpec((channels, GROUP), lambda i: (0, i)),
            pl.BlockSpec((channels, GROUP), lambda i: (0, groups + i)),
            pl.BlockSpec((channels, GROUP), lambda i: (0, 2 * groups + i)),
            pl.BlockSpec((strip, features), lambda i: (strip_at, 0), pipeline_mode=once),
            pl.BlockSpec(w_obs.shape, whole, pipeline_mode=once),
            pl.BlockSpec(w_out.shape, whole, pipeline_mode=once),
            pl.BlockSpec((1, GROUP), lambda i: (0, i)),
            pl.BlockSpec((heads, CELLS, CELLS), lambda i: (i, 0, 0)),
            pl.BlockSpec((1, features), whole),
        ],
        out_specs=[
            pl.BlockSpec((size, features), whole),
            pl.BlockSpec((size, features), whole),
            pl.BlockSpec((EDGE, features), whole),
            pl.BlockSpec((EDGE, features), whole),
        ],
        out_shape=[
            jax.ShapeDtypeStruct((size, features), BF16),
            jax.ShapeDtypeStruct((size, features), BF16),
            jax.ShapeDtypeStruct((EDGE, features), BF16),
            jax.ShapeDtypeStruct((EDGE, features), BF16),
        ],
        scratch_shapes=[
            pltpu.VMEM((strip, 2 * channels), BF16),
            pltpu.VMEM((groups, strip, GROUP), BF16),
            pltpu.VMEM((strip, features), BF16),
        ],
        compiler_params=pltpu.CompilerParams(vmem_limit_bytes=48 * 1024 * 1024),
        cost_estimate=pl.CostEstimate(
            flops=14 * strip * features * features,
            bytes_accessed=12 * strip * features + 8 * features * features,
            transcendentals=strip * CELLS * bias.shape[0],
        ),
    )(
        targets, rows, base, base, base, folded, folded, folded, ordered, w_obs, w_out, scale, bias, gain
    )


def join_kernel(lon_cells, *refs):
    ins, out_ref = refs[:-1], refs[-1]
    count = len(ins) // 2
    size = ins[0].shape[0]
    row = lax.broadcasted_iota(jnp.int32, (size, 1), 0)
    line, lon = divided(row, lon_cells)
    edge = jnp.where(lon < HALF_O, line * HALF_O + lon, -1)
    insert = (edge == lax.broadcasted_iota(jnp.int32, (1, EDGE), 1)).astype(F32).astype(BF16)
    for at in range(count):

        @pl.when(pl.program_id(0) == at)
        def _():
            west = dot(insert, ins[2 * at + 1][...]).astype(BF16)
            full = jnp.where(lon < HALF_O, west.astype(F32), ins[2 * at][...].astype(F32)).astype(BF16)
            half = size // WL
            for l in range(WL):
                out_ref[l, 0] = full[l * half : (l + 1) * half]


def join(pairs, lon_cells):
    size, features = pairs[0][0].shape
    whole = lambda i: (0, 0)
    specs = []
    flat = []
    for block, edge in pairs:
        specs += [pl.BlockSpec((size, features), whole), pl.BlockSpec((EDGE, features), whole)]
        flat += [block, edge]
    return pl.pallas_call(
        functools.partial(join_kernel, lon_cells),
        grid=(len(pairs),),
        in_specs=specs,
        out_specs=pl.BlockSpec((WL, 1, size // WL, features), lambda i: (0, i, 0, 0)),
        out_shape=jax.ShapeDtypeStruct((WL, len(pairs), size // WL, features), BF16),
        compiler_params=pltpu.CompilerParams(vmem_limit_bytes=40 * 1024 * 1024),
        cost_estimate=pl.CostEstimate(
            flops=0, bytes_accessed=4 * len(pairs) * size * features, transcendentals=0
        ),
    )(*flat)


def body(
    latent_state,
    obs_rows,
    obs_cells,
    obs_counts,
    w_obs,
    w_qkv,
    w_out,
    logit_scale,
    pos_bias,
    out_gain,
):
    levels, lat_cells, lon_cells, features = latent_state.shape
    lat_devices = lax.axis_size("lat")
    lon_devices = lax.axis_size("lon")
    devices = lat_devices * lon_devices
    both = ("lat", "lon")
    capacity = obs_rows.shape[2] // devices
    channels = obs_rows.shape[3]
    me = lax.axis_index("lat") * lon_devices + lax.axis_index("lon")

    rows = lax.all_to_all(
        obs_rows.reshape(devices, capacity, channels), both, split_axis=0, concat_axis=0, tiled=True
    ).reshape(devices * capacity, channels)
    cells = lax.all_gather(obs_cells.reshape(1, devices * capacity), both, axis=0, tiled=True)
    counts = lax.all_gather(obs_counts.reshape(1, devices), both, axis=0, tiled=True)
    cells = lax.dynamic_slice(cells, (0, me * capacity), (devices, capacity))
    counts = lax.dynamic_slice(counts, (0, me), (devices, 1))
    live = jnp.arange(capacity, dtype=jnp.int32)[None, :] < counts
    targets = jnp.where(live, cells, -1).reshape(1, devices * capacity)

    base, folded, ordered = project(
        latent_state.reshape(-1, features), w_obs, w_qkv, lon_cells
    )
    scale = jnp.repeat(logit_scale * LOG2E, features // logit_scale.shape[0])[None]
    gain = out_gain[None]

    def attend(strip_at):
        return attend_strip(
            strip_at, targets, rows, base, folded, ordered, w_obs, w_out, scale, pos_bias, gain,
            lat_cells, lon_cells,
        )

    south = [(i, i + 1) for i in range(lat_devices - 1)]
    east = [(i, (i + 1) % lon_devices) for i in range(lon_devices)]
    south_east = [
        (a * lon_devices + o, b * lon_devices + p) for a, b in south for o, p in east
    ]
    low_near, low_far, low_near_edge, low_far_edge = attend(1)
    first = lax.ppermute(low_far, "lat", south)
    first_edge = lax.ppermute(low_far_edge, both, south_east)
    last_edge = lax.ppermute(low_near_edge, "lon", east)
    top_near, top_far, top_near_edge, top_far_edge = attend(0)
    second_edge = lax.ppermute(top_near_edge, "lon", east)
    third_edge = lax.ppermute(top_far_edge, "lon", east)
    joined = join(
        [
            (first, first_edge),
            (top_near, second_edge),
            (top_far, third_edge),
            (low_near, last_edge),
        ],
        lon_cells,
    )
    return joined.reshape(levels, lat_cells, lon_cells, features)


def solution(mesh):
    in_specs = (
        P(None, "lat", "lon", None),
        P("lat", "lon", None, None),
        P("lat", "lon", None),
        P("lat", "lon", None),
        P(),
        P(),
        P(),
        P(),
        P(),
        P(),
    )
    out_specs = P(None, "lat", "lon", None)
    return jax.shard_map(body, mesh=mesh, in_specs=in_specs, out_specs=out_specs, check_vma=False)
```

```python
import functools
import math

import jax
import jax.numpy as jnp
from jax import lax
from jax.experimental import pallas as pl
from jax.experimental.pallas import tpu as pltpu
from jax.sharding import PartitionSpec as P

WL = 2
WA = 12
WO = 6
CELLS = WL * WA * WO
HALF_A = WA // 2
HALF_O = WO // 2
GROUP = 256
EDGE = 48

cosine_eps = 1e-06
layer_eps = 1e-05
LOG2E = math.log2(math.e)
VMEM_LIMIT = 56 * 1024 * 1024

F32 = jnp.float32
BF16 = jnp.bfloat16


def divided(x, n):
    quotient = lax.div(x, jnp.full_like(x, n))
    return quotient, x - quotient * n


def window_parts(row):
    window, inner = divided(row, CELLS)
    level, inner = divided(inner, WA * WO)
    lat, lon = divided(inner, WO)
    return window, level, lat, lon


def dot(a, b):
    return jnp.dot(a, b, preferred_element_type=F32)


def selection(rows, columns):
    return (rows == columns).astype(F32).astype(BF16)


def project_kernel(
    lon_cells, latent_ref, w_obs_ref, wq_ref, wk_ref, wv_ref, base_ref, folded_ref, ordered_ref, left
):
    rows = latent_ref.shape[0]
    strip = WL * WA * lon_cells
    strips = rows // strip
    part = WA * lon_cells

    @pl.when(pl.program_id(0) == 0)
    def _():
        row = lax.broadcasted_iota(jnp.int32, (strip, 1), 0)
        window, level, lat, lon = window_parts(row)
        source = level * part + lat * lon_cells + window * WO + lon
        perm = selection(source, lax.broadcasted_iota(jnp.int32, (1, strip), 1))
        for s in range(strips):
            cells = jnp.concatenate(
                [
                    latent_ref[l * strips * part + s * part : l * strips * part + (s + 1) * part]
                    for l in range(WL)
                ],
                axis=0,
            )
            moved = dot(perm, cells).astype(BF16)
            left[s * strip : (s + 1) * strip] = moved
            ordered_ref[s * strip : (s + 1) * strip] = moved
        left[rows:] = w_obs_ref[...]

    for i, w_ref in enumerate((wq_ref, wk_ref, wv_ref)):
        result = dot(left[...], w_ref[...])
        base_ref[0, i] = result[:rows]
        folded_ref[0, i] = result[rows:].astype(BF16)


def project(latent, w_obs, w_qkv, lon_cells):
    rows, features = latent.shape
    channels = w_obs.shape[0]
    columns = w_qkv.shape[1]
    groups = features // GROUP
    whole = lambda i: (0, 0)
    return pl.pallas_call(
        functools.partial(project_kernel, lon_cells),
        grid=(groups,),
        in_specs=[
            pl.BlockSpec((rows, features), whole, pipeline_mode=pl.Buffered(buffer_count=1)),
            pl.BlockSpec((channels, features), whole, pipeline_mode=pl.Buffered(buffer_count=1)),
            pl.BlockSpec((features, GROUP), lambda i: (0, i)),
            pl.BlockSpec((features, GROUP), lambda i: (0, groups + i)),
            pl.BlockSpec((features, GROUP), lambda i: (0, 2 * groups + i)),
        ],
        out_specs=[
            pl.BlockSpec((1, 3, rows, GROUP), lambda i: (i, 0, 0, 0)),
            pl.BlockSpec((1, 3, channels, GROUP), lambda i: (i, 0, 0, 0)),
            pl.BlockSpec((rows, features), whole),
        ],
        out_shape=[
            jax.ShapeDtypeStruct((groups, 3, rows, GROUP), F32),
            jax.ShapeDtypeStruct((groups, 3, channels, GROUP), BF16),
            jax.ShapeDtypeStruct((rows, features), BF16),
        ],
        scratch_shapes=[pltpu.VMEM((rows + channels, features), BF16)],
        compiler_params=pltpu.CompilerParams(vmem_limit_bytes=VMEM_LIMIT),
        cost_estimate=pl.CostEstimate(
            flops=2 * (rows + channels) * features * columns,
            bytes_accessed=4 * rows * columns + 2 * features * columns + 4 * rows * features,
            transcendentals=0,
        ),
    )(latent, w_obs, w_qkv, w_qkv, w_qkv)


def windows_kernel(
    strip_at,
    first,
    lon_cells,
    lat_cells,
    edges,
    targets_ref,
    scale_ref,
    gain_ref,
    rows_hbm,
    base_hbm,
    folded_hbm,
    ordered_hbm,
    w_obs_hbm,
    w_out_hbm,
    bias_hbm,
    near_ref,
    far_ref,
    *rest,
):
    edge_refs = rest[:edges]
    rows_ref, base_ref, folded_ref, ordered_ref, w_obs_ref, w_out_ref, bias_ref, context, sems = rest[
        edges:
    ]
    count, features = ordered_ref.shape
    windows = count // CELLS
    groups = base_ref.shape[0]
    heads = bias_ref.shape[0] // groups
    width = GROUP // heads
    slots = targets_ref.shape[1]
    chunk = 1024
    start = (strip_at * (lon_cells // WO) + first) * CELLS
    mine = pl.ds(start, count)

    copies = [pltpu.make_async_copy(rows_hbm, rows_ref, sems.at[0])]
    for g in range(groups):
        copies.append(
            pltpu.make_async_copy(base_hbm.at[g, :, mine], base_ref.at[g], sems.at[1 + 3 * g])
        )
        copies.append(
            pltpu.make_async_copy(folded_hbm.at[g], folded_ref.at[g], sems.at[2 + 3 * g])
        )
        some = pl.ds(g * heads, heads)
        copies.append(
            pltpu.make_async_copy(bias_hbm.at[some], bias_ref.at[some], sems.at[3 + 3 * g])
        )
    last = 1 + 3 * groups
    copies.append(pltpu.make_async_copy(ordered_hbm.at[mine], ordered_ref, sems.at[last]))
    copies.append(pltpu.make_async_copy(w_obs_hbm, w_obs_ref, sems.at[last + 1]))
    copies.append(pltpu.make_async_copy(w_out_hbm, w_out_ref, sems.at[last + 2]))
    for copy in copies:
        copy.start()

    row = lax.broadcasted_iota(jnp.int32, (count, 1), 0)
    window, level, lat, lon = window_parts(row)
    cell = (level * lat_cells + strip_at * WA + lat) * lon_cells + (first + window) * WO + lon
    copies[0].wait()
    total = jnp.zeros((count, rows_ref.shape[1]), F32)
    for at in range(0, slots, chunk):
        total += dot(selection(cell, targets_ref[:, at : at + chunk]), rows_ref[at : at + chunk])
    high = total.astype(BF16)
    low = (total - high.astype(F32)).astype(BF16)

    lane = lax.broadcasted_iota(jnp.int32, (1, GROUP), 1)
    same_head = selection(
        lax.broadcasted_iota(jnp.int32, (GROUP, 1), 0) // width, lane // width
    )
    left_half = lax.broadcasted_iota(jnp.int32, (CELLS, 2 * width), 1) < width
    blank = jnp.zeros((width, CELLS), BF16)

    def projected(g):
        for copy in copies[1 + 3 * g : 4 + 3 * g]:
            copy.wait()
        query, keys, values = (
            base_ref[g, i] + dot(high, folded_ref[g, i]) for i in range(3)
        )
        query_sum = dot((query * query).astype(BF16), same_head)
        keys_sum = dot((keys * keys).astype(BF16), same_head)
        scale = scale_ref[:, g * GROUP : (g + 1) * GROUP]
        query_n = (query * (lax.rsqrt(query_sum + cosine_eps) * scale)).astype(BF16)
        keys_n = keys * lax.rsqrt(keys_sum + cosine_eps)
        keys_t = [
            keys_n[w * CELLS : (w + 1) * CELLS].T.astype(BF16) for w in range(windows)
        ]
        return query_n, keys_t, values

    def attended(g, query_n, keys_t, values):
        for w in range(windows):
            here = slice(w * CELLS, (w + 1) * CELLS)
            for pair in range(heads // 2):
                lanes = slice(2 * pair * width, 2 * (pair + 1) * width)
                query_p = query_n[here, lanes]
                keys_p = keys_t[w][lanes]
                values_p = values[here, lanes]
                sums = []
                for side in range(2):
                    picked = keys_p[side * width : (side + 1) * width]
                    picked = jnp.concatenate([blank, picked] if side else [picked, blank], axis=0)
                    scores = dot(query_p, picked)
                    expo = jnp.exp2(scores + bias_ref[g * heads + 2 * pair + side]).astype(BF16)
                    mixed = jnp.where(left_half == (side == 0), values_p, 1.0).astype(BF16)
                    sums.append(dot(expo, mixed))
                weighted = jnp.where(left_half, sums[0], sums[1])
                norm = pltpu.roll(jnp.where(left_half, sums[1], sums[0]), width, 1)
                at = g * GROUP + 2 * pair * width
                context[here, at : at + 2 * width] = (weighted / norm).astype(BF16)

    ready = projected(0)
    for g in range(groups):
        after = projected(g + 1) if g + 1 < groups else None
        attended(g, *ready)
        ready = after

    for copy in copies[last:]:
        copy.wait()
    proj = dot(context[...], w_out_ref[...])
    latent = ordered_ref[...].astype(F32) + dot(high, w_obs_ref[...]) + dot(low, w_obs_ref[...])
    center = proj - jnp.mean(proj, -1, keepdims=True)
    spread = jnp.mean(center * center, -1, keepdims=True)
    normed = center * lax.rsqrt(spread + layer_eps) * gain_ref[...]
    done = latent + normed
    run = HALF_A * WO
    halves = ([], [])
    for w in range(windows):
        for h, out_ref in enumerate((near_ref, far_ref)):
            runs = []
            for l in range(WL):
                at = w * CELLS + ((l - WL // 2) % WL) * WA * WO + h * run
                runs.append(done[at : at + run])
            half = jnp.concatenate(runs, axis=0).astype(BF16)
            out_ref[w] = half
    if edges:
        source = lax.broadcasted_iota(jnp.int32, (1, WL * run), 1)
        line, lon = divided(source, WO)
        edge = jnp.where(lon >= HALF_O, line * HALF_O + lon - HALF_O, -1)
        pick = selection(lax.broadcasted_iota(jnp.int32, (EDGE, 1), 0), edge)
        for h, out_ref in enumerate((near_ref, far_ref)):
            chosen = dot(pick, out_ref[windows - 1]).astype(BF16)
            if edges == 2:
                edge_refs[h][...] = chosen
            else:
                edge_refs[0][h * EDGE : (h + 1) * EDGE] = chosen


def attend_windows(
    strip_at, first, windows, edges, targets, scale, gain, rows, base, folded, ordered, w_obs, w_out,
    bias, lat_cells, lon_cells,
):
    count = windows * CELLS
    features = w_out.shape[0]
    groups = features // GROUP
    channels = w_obs.shape[0]
    half = jax.ShapeDtypeStruct((windows, CELLS // 2, features), BF16)
    outs = [half, half] + [
        jax.ShapeDtypeStruct((EDGE * 2 // edges, features), BF16) for _ in range(edges)
    ]
    here = pl.BlockSpec(memory_space=pltpu.VMEM)
    there = pl.BlockSpec(memory_space=pl.ANY)
    return pl.pallas_call(
        functools.partial(windows_kernel, strip_at, first, lon_cells, lat_cells, edges),
        in_specs=[here] * 3 + [there] * 7,
        out_specs=[here] * len(outs),
        out_shape=outs,
        scratch_shapes=[
            pltpu.VMEM(rows.shape, BF16),
            pltpu.VMEM((groups, 3, count, GROUP), F32),
            pltpu.VMEM((groups, 3, channels, GROUP), BF16),
            pltpu.VMEM((count, features), BF16),
            pltpu.VMEM(w_obs.shape, BF16),
            pltpu.VMEM(w_out.shape, BF16),
            pltpu.VMEM(bias.shape, F32),
            pltpu.VMEM((count, features), BF16),
            pltpu.SemaphoreType.DMA((4 + 3 * groups,)),
        ],
        compiler_params=pltpu.CompilerParams(vmem_limit_bytes=VMEM_LIMIT),
        cost_estimate=pl.CostEstimate(
            flops=14 * count * features * features,
            bytes_accessed=12 * count * features + 8 * features * features,
            transcendentals=count * CELLS * bias.shape[0],
        ),
    )(targets, scale, gain, rows, base, folded, ordered, w_obs, w_out, bias)


def join_kernel(lon_cells, count, *refs):
    ins, out_ref = refs[:-1], refs[-1]
    run = HALF_A * WO
    size = WL * HALF_A * lon_cells
    parts = len(ins) // count
    row = lax.broadcasted_iota(jnp.int32, (size, 1), 0)
    line, moved = divided(row, lon_cells)
    level, lat = divided(line, HALF_A)
    in_edge = moved < HALF_O
    window, lon = divided(jnp.maximum(moved - HALF_O, 0), WO)
    source = jnp.where(in_edge, -1, ((window * WL + level) * HALF_A + lat) * WO + lon)
    edge = jnp.where(in_edge, line * HALF_O + moved, -1)
    insert = selection(edge, lax.broadcasted_iota(jnp.int32, (1, EDGE), 1))
    for at in range(count):

        @pl.when(pl.program_id(0) == at)
        def _():
            mine = ins[at * parts : (at + 1) * parts]
            full = dot(insert, mine[-1][...])
            begin = 0
            for ref in mine[:-1]:
                held = ref.shape[0]
                index = lax.broadcasted_iota(jnp.int32, (1, held), 1) + begin
                full += dot(selection(source, index), ref[...])
                begin += held
            full = full.astype(BF16)
            half = size // WL
            for l in range(WL):
                out_ref[l, 0] = full[l * half : (l + 1) * half]


def join(blocks, lon_cells):
    features = blocks[0][0].shape[-1]
    size = WL * HALF_A * lon_cells
    whole = lambda i: (0, 0)
    flat = [part for block in blocks for part in block]
    return pl.pallas_call(
        functools.partial(join_kernel, lon_cells, len(blocks)),
        grid=(len(blocks),),
        in_specs=[pl.BlockSpec(part.shape, whole) for part in flat],
        out_specs=pl.BlockSpec((WL, 1, size // WL, features), lambda i: (0, i, 0, 0)),
        out_shape=jax.ShapeDtypeStruct((WL, len(blocks), size // WL, features), BF16),
        compiler_params=pltpu.CompilerParams(vmem_limit_bytes=VMEM_LIMIT),
        cost_estimate=pl.CostEstimate(
            flops=0, bytes_accessed=4 * len(blocks) * size * features, transcendentals=0
        ),
    )(*flat)


def body(
    latent_state,
    obs_rows,
    obs_cells,
    obs_counts,
    w_obs,
    w_qkv,
    w_out,
    logit_scale,
    pos_bias,
    out_gain,
):
    levels, lat_cells, lon_cells, features = latent_state.shape
    lat_devices = lax.axis_size("lat")
    lon_devices = lax.axis_size("lon")
    devices = lat_devices * lon_devices
    both = ("lat", "lon")
    capacity = obs_rows.shape[2] // devices
    channels = obs_rows.shape[3]

    rows = lax.all_to_all(
        obs_rows.reshape(devices, capacity, channels), both, split_axis=0, concat_axis=0, tiled=True
    ).reshape(devices * capacity, channels)
    live = jnp.arange(capacity, dtype=jnp.int32)[None, :] < obs_counts.reshape(devices, 1)
    cells = jnp.where(live, obs_cells.reshape(devices, capacity), -1)
    targets = lax.all_to_all(cells, both, split_axis=0, concat_axis=0, tiled=True)
    targets = targets.reshape(1, devices * capacity)

    base, folded, ordered = project(
        latent_state.reshape(-1, features), w_obs, w_qkv, lon_cells
    )
    scale = jnp.repeat(logit_scale * LOG2E, features // logit_scale.shape[0])[None]
    bias = pos_bias * LOG2E
    gain = out_gain[None]
    half_windows = lon_cells // WO // 2
    held = half_windows * CELLS // 2

    def attend(strip_at, part, edges):
        near, far, *others = attend_windows(
            strip_at, part * half_windows, half_windows, edges, targets, scale, gain, rows, base,
            folded, ordered, w_obs, w_out, bias, lat_cells, lon_cells,
        )
        return [near.reshape(held, features), far.reshape(held, features), *others]

    south = [(i, i + 1) for i in range(lat_devices - 1)]
    east = [(i, (i + 1) % lon_devices) for i in range(lon_devices)]
    south_east = [
        (a * lon_devices + o, b * lon_devices + p) for a, b in south for o, p in east
    ]
    low_near_1, low_far_1, low_near_edge, low_far_edge = attend(1, 1, 2)
    first_1 = lax.ppermute(low_far_1, "lat", south)
    first_edge = lax.ppermute(low_far_edge, both, south_east)
    last_edge = lax.ppermute(low_near_edge, "lon", east)
    low_near_0, low_far_0 = attend(1, 0, 0)
    first_0 = lax.ppermute(low_far_0, "lat", south)
    top_near_1, top_far_1, top_edges = attend(0, 1, 1)
    top_edges = lax.ppermute(top_edges, "lon", east)
    top_near_0, top_far_0 = attend(0, 0, 0)
    joined = join(
        [
            (first_0, first_1, first_edge),
            (top_near_0, top_near_1, top_edges[:EDGE]),
            (top_far_0, top_far_1, top_edges[EDGE:]),
            (low_near_0, low_near_1, last_edge),
        ],
        lon_cells,
    )
    return joined.reshape(levels, lat_cells, lon_cells, features)


def solution(mesh):
    in_specs = (
        P(None, "lat", "lon", None),
        P("lat", "lon", None, None),
        P("lat", "lon", None),
        P("lat", "lon", None),
        P(),
        P(),
        P(),
        P(),
        P(),
        P(),
    )
    out_specs = P(None, "lat", "lon", None)
    return jax.shard_map(body, mesh=mesh, in_specs=in_specs, out_specs=out_specs, check_vma=False)
```

```python
import functools
import math

import jax
import jax.numpy as jnp
from jax import lax
from jax.experimental import pallas as pl
from jax.experimental.pallas import tpu as pltpu
from jax.sharding import PartitionSpec as P

WL = 2
WA = 12
WO = 6
CELLS = WL * WA * WO
HALF_A = WA // 2
HALF_O = WO // 2
GROUP = 256
EXTRA = 8
BLOCK = 32
DIGIT = 32
DEAD = 255
EDGE = 48

cosine_eps = 1e-06
layer_eps = 1e-05
LOG2E = math.log2(math.e)
VMEM_LIMIT = 56 * 1024 * 1024

F32 = jnp.float32
BF16 = jnp.bfloat16


def divided(x, n):
    quotient = lax.div(x, jnp.full_like(x, n))
    return quotient, x - quotient * n


def window_parts(row):
    window, inner = divided(row, CELLS)
    level, inner = divided(inner, WA * WO)
    lat, lon = divided(inner, WO)
    return window, level, lat, lon


def dot(a, b):
    return jnp.dot(a, b, preferred_element_type=F32)


def selection(rows, columns):
    return (rows == columns).astype(F32).astype(BF16)


def pack_kernel(rows_ref, cells_ref, counts_ref, packed_ref):
    devices, capacity, channels = rows_ref.shape
    slots = devices * capacity
    packed_ref[:, :capacity] = rows_ref[...]
    cells = cells_ref[...]
    high = lax.div(cells, jnp.full_like(cells, DIGIT))
    low = cells - high * DIGIT
    slot = lax.broadcasted_iota(jnp.int32, (1, slots), 1)
    device = lax.broadcasted_iota(jnp.int32, (devices, 1), 0)
    place = lax.broadcasted_iota(jnp.int32, (slots, 1), 0)
    place = lax.rem(place, jnp.full_like(place, capacity))
    lane = lax.broadcasted_iota(jnp.int32, (1, channels), 1)
    own = divided(slot, capacity)[0] == device
    digits = jnp.zeros((devices, channels), F32)
    for i, digit in enumerate((high, low)):
        spread = jnp.where(own, digit.astype(F32), 0.0).astype(BF16)
        digits += dot(spread, selection(place + i * capacity, lane))
    same = device == lax.broadcasted_iota(jnp.int32, (1, devices), 1)
    count = jnp.sum(jnp.where(same, counts_ref[...].astype(F32), 0.0), -1, keepdims=True)
    dead = (lane < capacity) & (lane.astype(F32) >= count)
    digits = jnp.where(dead, float(DEAD), digits)
    packed_ref[:, capacity:] = jnp.broadcast_to(
        digits[:, None, :], (devices, EXTRA, channels)
    ).astype(BF16)


def pack(rows, cells, counts):
    devices, capacity, channels = rows.shape
    return pl.pallas_call(
        pack_kernel,
        out_shape=jax.ShapeDtypeStruct((devices, capacity + EXTRA, channels), BF16),
        compiler_params=pltpu.CompilerParams(vmem_limit_bytes=VMEM_LIMIT),
    )(rows, cells, counts)


def project_kernel(
    lon_cells,
    latent_ref,
    w_obs_ref,
    wq_ref,
    wk_ref,
    wv_ref,
    bias_ref,
    base_ref,
    folded_ref,
    ordered_ref,
    scaled_ref,
    left,
):
    rows = latent_ref.shape[0]
    strip = WL * WA * lon_cells
    strips = rows // strip
    part = WA * lon_cells

    @pl.when(pl.program_id(0) == 0)
    def _():
        row = lax.broadcasted_iota(jnp.int32, (strip, 1), 0)
        window, level, lat, lon = window_parts(row)
        source = level * part + lat * lon_cells + window * WO + lon
        perm = selection(source, lax.broadcasted_iota(jnp.int32, (1, strip), 1))
        for s in range(strips):
            cells = jnp.concatenate(
                [
                    latent_ref[l * strips * part + s * part : l * strips * part + (s + 1) * part]
                    for l in range(WL)
                ],
                axis=0,
            )
            moved = dot(perm, cells).astype(BF16)
            left[s * strip : (s + 1) * strip] = moved
            ordered_ref[s * strip : (s + 1) * strip] = moved
        left[rows:] = w_obs_ref[...]

    for i, w_ref in enumerate((wq_ref, wk_ref, wv_ref)):
        result = dot(left[...], w_ref[...])
        base_ref[0, i] = result[:rows]
        folded_ref[0, i] = result[rows:].astype(BF16)
    scaled_ref[...] = bias_ref[...] * LOG2E


def project(latent, w_obs, w_qkv, bias, lon_cells):
    rows, features = latent.shape
    channels = w_obs.shape[0]
    columns = w_qkv.shape[1]
    groups = features // GROUP
    heads = bias.shape[0] // groups
    whole = lambda i: (0, 0)
    once = pl.Buffered(buffer_count=1)
    some_heads = pl.BlockSpec((heads, CELLS, CELLS), lambda i: (i, 0, 0))
    return pl.pallas_call(
        functools.partial(project_kernel, lon_cells),
        grid=(groups,),
        in_specs=[
            pl.BlockSpec((rows, features), whole, pipeline_mode=once),
            pl.BlockSpec((channels, features), whole, pipeline_mode=once),
            pl.BlockSpec((features, GROUP), lambda i: (0, i)),
            pl.BlockSpec((features, GROUP), lambda i: (0, groups + i)),
            pl.BlockSpec((features, GROUP), lambda i: (0, 2 * groups + i)),
            some_heads,
        ],
        out_specs=[
            pl.BlockSpec((1, 3, rows, GROUP), lambda i: (i, 0, 0, 0)),
            pl.BlockSpec((1, 3, channels, GROUP), lambda i: (i, 0, 0, 0)),
            pl.BlockSpec((rows, features), whole),
            some_heads,
        ],
        out_shape=[
            jax.ShapeDtypeStruct((groups, 3, rows, GROUP), F32),
            jax.ShapeDtypeStruct((groups, 3, channels, GROUP), BF16),
            jax.ShapeDtypeStruct((rows, features), BF16),
            jax.ShapeDtypeStruct(bias.shape, F32),
        ],
        scratch_shapes=[pltpu.VMEM((rows + channels, features), BF16)],
        compiler_params=pltpu.CompilerParams(vmem_limit_bytes=VMEM_LIMIT),
        cost_estimate=pl.CostEstimate(
            flops=2 * (rows + channels) * features * columns,
            bytes_accessed=4 * rows * columns + 2 * features * columns + 4 * rows * features,
            transcendentals=0,
        ),
    )(latent, w_obs, w_qkv, w_qkv, w_qkv, bias)


def strip_kernel(
    strip_at,
    lon_cells,
    lat_cells,
    passed,
    packed_ref,
    scale_ref,
    gain_ref,
    base_ref,
    folded_ref,
    bias_ref,
    ordered_hbm,
    w_obs_hbm,
    w_out_hbm,
    *rest,
):
    rest = list(rest)
    carried_ref = rest.pop(0) if passed else None
    near_ref, far_ref = rest.pop(0), rest.pop(0)
    edge_refs = [rest.pop(0) for _ in range(1 if passed else 2)]
    ordered_ref, w_obs_ref, w_out_ref, gathered, context, sems = rest
    step = pl.program_id(0)
    strip, features = ordered_ref.shape
    windows = strip // CELLS
    groups = features // GROUP
    heads = bias_ref.shape[0]
    width = GROUP // heads
    devices, held, channels = packed_ref.shape
    capacity = held - EXTRA
    copies = [
        pltpu.make_async_copy(ordered_hbm.at[pl.ds(strip_at * strip, strip)], ordered_ref, sems.at[0]),
        pltpu.make_async_copy(w_obs_hbm, w_obs_ref, sems.at[1]),
        pltpu.make_async_copy(w_out_hbm, w_out_ref, sems.at[2]),
    ]

    @pl.when(step == 0)
    def _():
        for copy in copies:
            copy.start()
        row = lax.broadcasted_iota(jnp.int32, (strip, 1), 0)
        window, level, lat, lon = window_parts(row)
        cell = (level * lat_cells + strip_at * WA + lat) * lon_cells + window * WO + lon
        count = BLOCK * capacity
        slot = lax.broadcasted_iota(jnp.int32, (1, count), 1)
        source, place = divided(slot, capacity)
        lane = lax.broadcasted_iota(jnp.int32, (channels, 1), 0)
        weigh = jnp.where(lane == place, float(DIGIT), 0.0) + jnp.where(
            lane == place + capacity, 1.0, 0.0
        )
        line = lax.broadcasted_iota(jnp.int32, (BLOCK * EXTRA, 1), 0)
        total = jnp.zeros((strip, channels), F32)
        for at in range(0, devices, BLOCK):
            digits = packed_ref[at : at + BLOCK, capacity:].reshape(BLOCK * EXTRA, channels)
            values = dot(digits, weigh.astype(BF16))
            target = jnp.sum(
                jnp.where(line == source * EXTRA, values, 0.0), 0, keepdims=True
            )
            rows = packed_ref[at : at + BLOCK, :capacity].reshape(count, channels)
            total += dot(selection(cell, target.astype(jnp.int32)), rows)
        high = total.astype(BF16)
        gathered[0] = high
        gathered[1] = (total - high.astype(F32)).astype(BF16)

    lane_head = lax.broadcasted_iota(jnp.int32, (1, GROUP), 1) // width
    same_head = selection(lax.broadcasted_iota(jnp.int32, (GROUP, 1), 0) // width, lane_head)
    scale = jnp.zeros((1, GROUP), F32)
    for h in range(heads):
        scale = jnp.where(lane_head == h, scale_ref[step * heads + h] * LOG2E, scale)
    left_half = lax.broadcasted_iota(jnp.int32, (CELLS, 2 * width), 1) < width
    blank = jnp.zeros((width, CELLS), BF16)

    high = gathered[0]
    query, keys, values = (base_ref[0, i] + dot(high, folded_ref[0, i]) for i in range(3))
    query_sum = dot((query * query).astype(BF16), same_head)
    keys_sum = dot((keys * keys).astype(BF16), same_head)
    query_n = (query * (lax.rsqrt(query_sum + cosine_eps) * scale)).astype(BF16)
    keys_n = keys * lax.rsqrt(keys_sum + cosine_eps)

    def scored(w):
        here = slice(w * CELLS, (w + 1) * CELLS)
        keys_t = keys_n[here].T.astype(BF16)
        result = []
        for h in range(heads):
            pair, side = h // 2, h % 2
            lanes = slice(2 * pair * width, 2 * (pair + 1) * width)
            picked = keys_t[h * width : (h + 1) * width]
            picked = jnp.concatenate([blank, picked] if side else [picked, blank], axis=0)
            result.append(dot(query_n[here, lanes], picked))
        return result

    def weighted(w, scores):
        here = slice(w * CELLS, (w + 1) * CELLS)
        expo = [jnp.exp2(scores[h] + bias_ref[h]).astype(BF16) for h in range(heads)]
        sums = []
        for h in range(heads):
            lanes = slice(h // 2 * 2 * width, (h // 2 + 1) * 2 * width)
            mixed = jnp.where(left_half == (h % 2 == 0), values[here, lanes], 1.0).astype(BF16)
            sums.append(dot(expo[h], mixed))
        parts = []
        for a, b in zip(sums[::2], sums[1::2]):
            norm = pltpu.roll(jnp.where(left_half, b, a), width, 1)
            parts.append(jnp.where(left_half, a, b) / norm)
        context[step, here] = jnp.concatenate(parts, axis=1).astype(BF16)

    scores = scored(0)
    for w in range(windows):
        after = scored(w + 1) if w + 1 < windows else None
        weighted(w, scores)
        scores = after

    @pl.when(step == groups - 1)
    def _():
        for copy in copies:
            copy.wait()
        pieces = 2
        size = strip // pieces
        cuts = [slice(at * size, (at + 1) * size) for at in range(pieces)]
        projs = [
            dot(jnp.concatenate([context[g, cut] for g in range(groups)], axis=1), w_out_ref[...])
            for cut in cuts
        ]
        latents = [
            ordered_ref[cut].astype(F32)
            + dot(gathered[0, cut], w_obs_ref[...])
            + dot(gathered[1, cut], w_obs_ref[...])
            for cut in cuts
        ]
        done = []
        for proj, latent in zip(projs, latents):
            center = proj - jnp.mean(proj, -1, keepdims=True)
            spread = jnp.mean(center * center, -1, keepdims=True)
            normed = center * lax.rsqrt(spread + layer_eps) * gain_ref[...]
            done.append((latent + normed).astype(BF16))
        done = jnp.concatenate(done, axis=0)
        row = lax.broadcasted_iota(jnp.int32, (1, strip), 1)
        window, level, lat, lon = window_parts(row)
        level = lax.rem(level + WL // 2, jnp.full_like(level, WL))
        half, lat = divided(lat, HALF_A)
        lon = window * WO + lon
        moved = lax.rem(lon + HALF_O, jnp.full_like(lon, lon_cells))
        place = ((half * WL + level) * HALF_A + lat) * lon_cells + moved
        edge = (level * HALF_A + lat) * HALF_O + moved
        size = WL * HALF_A * lon_cells
        for h, out_ref in enumerate((near_ref, far_ref)):
            index = lax.broadcasted_iota(jnp.int32, (size, 1), 0) + h * size
            out_ref[...] = dot(selection(index, place), done).astype(BF16)
            index = lax.broadcasted_iota(jnp.int32, (EDGE, 1), 0)
            wanted = jnp.where((moved < HALF_O) & (half == h), edge, -1)
            chosen = dot(selection(index, wanted), done).astype(BF16)
            if passed:
                edge_refs[0][h * EDGE : (h + 1) * EDGE] = chosen
            else:
                edge_refs[h][...] = chosen
        if passed:
            edge_refs[0][2 * EDGE :] = carried_ref[...]


def attend_strip(
    strip_at, packed, scale, gain, base, folded, bias, ordered, w_obs, w_out, lat_cells, lon_cells,
    carried=None,
):
    strip = WL * WA * lon_cells
    features = w_out.shape[0]
    groups = features // GROUP
    channels = w_obs.shape[0]
    heads = bias.shape[0] // groups
    passed = carried is not None
    whole = lambda i: (0, 0)
    once = pl.Buffered(buffer_count=1)
    there = pl.BlockSpec(memory_space=pl.ANY)
    half = (strip // 2, features)
    edges = [(3 * EDGE, features)] if passed else [(EDGE, features)] * 2
    outs = [half, half] + edges
    extra = [carried] if passed else []
    return pl.pallas_call(
        functools.partial(strip_kernel, strip_at, lon_cells, lat_cells, passed),
        grid=(groups,),
        in_specs=[
            pl.BlockSpec(packed.shape, lambda i: (0, 0, 0), pipeline_mode=once),
            pl.BlockSpec(memory_space=pltpu.SMEM),
            pl.BlockSpec((1, features), whole),
            pl.BlockSpec((1, 3, strip, GROUP), lambda i: (i, 0, strip_at, 0)),
            pl.BlockSpec((1, 3, channels, GROUP), lambda i: (i, 0, 0, 0)),
            pl.BlockSpec((heads, CELLS, CELLS), lambda i: (i, 0, 0)),
            there,
            there,
            there,
        ]
        + [pl.BlockSpec(part.shape, whole, pipeline_mode=once) for part in extra],
        out_specs=[pl.BlockSpec(shape, whole) for shape in outs],
        out_shape=[jax.ShapeDtypeStruct(shape, BF16) for shape in outs],
        scratch_shapes=[
            pltpu.VMEM((strip, features), BF16),
            pltpu.VMEM(w_obs.shape, BF16),
            pltpu.VMEM(w_out.shape, BF16),
            pltpu.VMEM((2, strip, channels), BF16),
            pltpu.VMEM((groups, strip, GROUP), BF16),
            pltpu.SemaphoreType.DMA((3,)),
        ],
        compiler_params=pltpu.CompilerParams(vmem_limit_bytes=VMEM_LIMIT),
        cost_estimate=pl.CostEstimate(
            flops=14 * strip * features * features,
            bytes_accessed=12 * strip * features + 8 * features * features,
            transcendentals=strip * CELLS * bias.shape[0],
        ),
    )(packed, scale, gain, base, folded, bias, ordered, w_obs, w_out, *extra)


def join_kernel(lon_cells, count, *refs):
    ins, out_ref = refs[:-1], refs[-1]
    size = WL * HALF_A * lon_cells
    row = lax.broadcasted_iota(jnp.int32, (size, 1), 0)
    line, moved = divided(row, lon_cells)
    edge = jnp.where(moved < HALF_O, line * HALF_O + moved, -1)
    insert = selection(edge, lax.broadcasted_iota(jnp.int32, (1, EDGE), 1))
    for at in range(count):

        @pl.when(pl.program_id(0) == at)
        def _():
            block_ref, edge_ref = ins[2 * at : 2 * at + 2]
            west = dot(insert, edge_ref[...])
            full = jnp.where(moved < HALF_O, west, block_ref[...].astype(F32)).astype(BF16)
            half = size // WL
            for l in range(WL):
                out_ref[l, 0] = full[l * half : (l + 1) * half]


def join(blocks, lon_cells):
    features = blocks[0][0].shape[-1]
    size = WL * HALF_A * lon_cells
    flat, specs = [], []
    for block, edges, at in blocks:
        flat += [block, edges]
        specs.append(pl.BlockSpec((size, features), lambda i: (0, 0)))
        specs.append(pl.BlockSpec((EDGE, features), lambda i, at=at: (at, 0)))
    return pl.pallas_call(
        functools.partial(join_kernel, lon_cells, len(blocks)),
        grid=(len(blocks),),
        in_specs=specs,
        out_specs=pl.BlockSpec((WL, 1, size // WL, features), lambda i: (0, i, 0, 0)),
        out_shape=jax.ShapeDtypeStruct((WL, len(blocks), size // WL, features), BF16),
        compiler_params=pltpu.CompilerParams(vmem_limit_bytes=VMEM_LIMIT),
        cost_estimate=pl.CostEstimate(
            flops=0, bytes_accessed=4 * len(blocks) * size * features, transcendentals=0
        ),
    )(*flat)


def body(
    latent_state,
    obs_rows,
    obs_cells,
    obs_counts,
    w_obs,
    w_qkv,
    w_out,
    logit_scale,
    pos_bias,
    out_gain,
):
    levels, lat_cells, lon_cells, features = latent_state.shape
    lat_devices = lax.axis_size("lat")
    lon_devices = lax.axis_size("lon")
    devices = lat_devices * lon_devices
    both = ("lat", "lon")
    capacity = obs_rows.shape[2] // devices
    channels = obs_rows.shape[3]

    packed = pack(
        obs_rows.reshape(devices, capacity, channels),
        obs_cells.reshape(1, devices * capacity),
        obs_counts.reshape(1, devices),
    )
    packed = lax.all_to_all(packed, both, split_axis=0, concat_axis=0, tiled=True)
    base, folded, ordered, bias = project(
        latent_state.reshape(-1, features), w_obs, w_qkv, pos_bias, lon_cells
    )
    gain = out_gain[None]

    def attend(strip_at, carried=None):
        return attend_strip(
            strip_at, packed, logit_scale, gain, base, folded, bias, ordered, w_obs, w_out,
            lat_cells, lon_cells, carried,
        )

    south = [(i, i + 1) for i in range(lat_devices - 1)]
    east = [(i, (i + 1) % lon_devices) for i in range(lon_devices)]
    south_east = [
        (a * lon_devices + o, b * lon_devices + p) for a, b in south for o, p in east
    ]
    low_near, low_far, low_near_edge, low_far_edge = attend(1)
    first = lax.ppermute(low_far, "lat", south)
    first_edge = lax.ppermute(low_far_edge, both, south_east)
    top_near, top_far, edges = attend(0, low_near_edge)
    edges, first_edge = lax.optimization_barrier((edges, first_edge))
    edges = lax.ppermute(edges, "lon", east)
    joined = join(
        [
            (first, first_edge, 0),
            (top_near, edges, 0),
            (top_far, edges, 1),
            (low_near, edges, 2),
        ],
        lon_cells,
    )
    return joined.reshape(levels, lat_cells, lon_cells, features)


def solution(mesh):
    in_specs = (
        P(None, "lat", "lon", None),
        P("lat", "lon", None, None),
        P("lat", "lon", None),
        P("lat", "lon", None),
        P(),
        P(),
        P(),
        P(),
        P(),
        P(),
    )
    out_specs = P(None, "lat", "lon", None)
    return jax.shard_map(body, mesh=mesh, in_specs=in_specs, out_specs=out_specs, check_vma=False)
```

```python
import functools
import math

import jax
import jax.numpy as jnp
from jax import lax
from jax.experimental import pallas as pl
from jax.experimental.pallas import tpu as pltpu
from jax.sharding import PartitionSpec as P

WL = 2
WA = 12
WO = 6
CELLS = WL * WA * WO
HALF_A = WA // 2
HALF_O = WO // 2
GROUP = 256
EXTRA = 8
BLOCK = 32
DIGIT = 32
DEAD = 255
EDGE = 48

cosine_eps = 1e-06
layer_eps = 1e-05
LOG2E = math.log2(math.e)
MIB = 1024 * 1024
LANES = 128

F32 = jnp.float32
BF16 = jnp.bfloat16


def divided(x, n):
    quotient = lax.div(x, jnp.full_like(x, n))
    return quotient, x - quotient * n


def window_parts(row):
    window, inner = divided(row, CELLS)
    level, inner = divided(inner, WA * WO)
    lat, lon = divided(inner, WO)
    return window, level, lat, lon


def dot(a, b):
    return jnp.dot(a, b, preferred_element_type=F32)


def selection(rows, columns):
    return (rows == columns).astype(F32).astype(BF16)


def pack_kernel(rows_ref, cells_ref, counts_ref, packed_ref):
    devices, capacity, channels = rows_ref.shape
    slots = devices * capacity
    for at in range(channels // LANES):
        part = rows_ref[:, :, at * LANES : (at + 1) * LANES]
        packed_ref[:, at * capacity : (at + 1) * capacity] = part
    cells = cells_ref[...]
    high = lax.div(cells, jnp.full_like(cells, DIGIT))
    low = cells - high * DIGIT
    slot = lax.broadcasted_iota(jnp.int32, (1, slots), 1)
    device = lax.broadcasted_iota(jnp.int32, (devices, 1), 0)
    place = lax.broadcasted_iota(jnp.int32, (slots, 1), 0)
    place = lax.rem(place, jnp.full_like(place, capacity))
    lane = lax.broadcasted_iota(jnp.int32, (1, LANES), 1)
    own = divided(slot, capacity)[0] == device
    digits = jnp.zeros((devices, LANES), F32)
    for i, digit in enumerate((high, low)):
        spread = jnp.where(own, digit.astype(F32), 0.0).astype(BF16)
        digits += dot(spread, selection(place + i * capacity, lane))
    same = device == lax.broadcasted_iota(jnp.int32, (1, devices), 1)
    count = jnp.sum(jnp.where(same, counts_ref[...].astype(F32), 0.0), -1, keepdims=True)
    dead = (lane < capacity) & (lane.astype(F32) >= count)
    digits = jnp.where(dead, float(DEAD), digits)
    packed_ref[:, channels // LANES * capacity :] = jnp.broadcast_to(
        digits[:, None, :], (devices, EXTRA, LANES)
    ).astype(BF16)


def pack(rows, cells, counts):
    devices, capacity, channels = rows.shape
    held = channels // LANES * capacity + EXTRA
    return pl.pallas_call(
        pack_kernel,
        out_shape=jax.ShapeDtypeStruct((devices, held, LANES), BF16),
        compiler_params=pltpu.CompilerParams(vmem_limit_bytes=16 * MIB),
    )(rows, cells, counts)


def project_kernel(
    lon_cells,
    latent_ref,
    w_obs_ref,
    wq_ref,
    wk_ref,
    wv_ref,
    bias_ref,
    base_ref,
    folded_ref,
    ordered_ref,
    scaled_ref,
    left,
):
    rows = latent_ref.shape[0]
    strip = WL * WA * lon_cells
    strips = rows // strip
    part = WA * lon_cells

    @pl.when(pl.program_id(0) == 0)
    def _():
        row = lax.broadcasted_iota(jnp.int32, (strip, 1), 0)
        window, level, lat, lon = window_parts(row)
        source = level * part + lat * lon_cells + window * WO + lon
        perm = selection(source, lax.broadcasted_iota(jnp.int32, (1, strip), 1))
        for s in range(strips):
            cells = jnp.concatenate(
                [
                    latent_ref[l * strips * part + s * part : l * strips * part + (s + 1) * part]
                    for l in range(WL)
                ],
                axis=0,
            )
            moved = dot(perm, cells).astype(BF16)
            left[s * strip : (s + 1) * strip] = moved
            ordered_ref[s * strip : (s + 1) * strip] = moved
        left[rows:] = w_obs_ref[...]

    for i, w_ref in enumerate((wq_ref, wk_ref, wv_ref)):
        result = dot(left[...], w_ref[...])
        base_ref[0, i] = result[:rows]
        folded_ref[0, i] = result[rows:].astype(BF16)
    scaled_ref[...] = bias_ref[...] * LOG2E


def project(latent, w_obs, w_qkv, bias, lon_cells):
    rows, features = latent.shape
    channels = w_obs.shape[0]
    columns = w_qkv.shape[1]
    groups = features // GROUP
    heads = bias.shape[0] // groups
    whole = lambda i: (0, 0)
    once = pl.Buffered(buffer_count=1)
    some_heads = pl.BlockSpec((heads, CELLS, CELLS), lambda i: (i, 0, 0))
    return pl.pallas_call(
        functools.partial(project_kernel, lon_cells),
        grid=(groups,),
        in_specs=[
            pl.BlockSpec((rows, features), whole, pipeline_mode=once),
            pl.BlockSpec((channels, features), whole, pipeline_mode=once),
            pl.BlockSpec((features, GROUP), lambda i: (0, i)),
            pl.BlockSpec((features, GROUP), lambda i: (0, groups + i)),
            pl.BlockSpec((features, GROUP), lambda i: (0, 2 * groups + i)),
            some_heads,
        ],
        out_specs=[
            pl.BlockSpec((1, 3, rows, GROUP), lambda i: (i, 0, 0, 0)),
            pl.BlockSpec((1, 3, channels, GROUP), lambda i: (i, 0, 0, 0)),
            pl.BlockSpec((rows, features), whole),
            some_heads,
        ],
        out_shape=[
            jax.ShapeDtypeStruct((groups, 3, rows, GROUP), F32),
            jax.ShapeDtypeStruct((groups, 3, channels, GROUP), BF16),
            jax.ShapeDtypeStruct((rows, features), BF16),
            jax.ShapeDtypeStruct(bias.shape, F32),
        ],
        scratch_shapes=[pltpu.VMEM((rows + channels, features), BF16)],
        compiler_params=pltpu.CompilerParams(vmem_limit_bytes=32 * MIB),
        cost_estimate=pl.CostEstimate(
            flops=2 * (rows + channels) * features * columns,
            bytes_accessed=4 * rows * columns + 2 * features * columns + 4 * rows * features,
            transcendentals=0,
        ),
    )(latent, w_obs, w_qkv, w_qkv, w_qkv, bias)


def strip_kernel(
    strip_at,
    lon_cells,
    lat_cells,
    passed,
    packed_ref,
    scale_ref,
    gain_ref,
    base_ref,
    folded_ref,
    bias_ref,
    ordered_hbm,
    w_obs_hbm,
    w_out_hbm,
    *rest,
):
    carried_ref = rest[0] if passed else None
    near_ref, far_ref, edge_ref, ordered_ref, w_obs_ref, w_out_ref, gathered, context, sems = rest[
        passed:
    ]
    step = pl.program_id(0)
    strip, features = ordered_ref.shape
    windows = strip // CELLS
    groups = features // GROUP
    heads = bias_ref.shape[0]
    width = GROUP // heads
    devices, held, _ = packed_ref.shape
    channels = w_obs_ref.shape[0]
    cuts = channels // LANES
    capacity = (held - EXTRA) // cuts
    copies = [
        pltpu.make_async_copy(ordered_hbm.at[pl.ds(strip_at * strip, strip)], ordered_ref, sems.at[0]),
        pltpu.make_async_copy(w_obs_hbm, w_obs_ref, sems.at[1]),
        pltpu.make_async_copy(w_out_hbm, w_out_ref, sems.at[2]),
    ]

    @pl.when(step == 0)
    def _():
        for copy in copies:
            copy.start()
        row = lax.broadcasted_iota(jnp.int32, (strip, 1), 0)
        window, level, lat, lon = window_parts(row)
        cell = (level * lat_cells + strip_at * WA + lat) * lon_cells + window * WO + lon
        count = BLOCK * capacity
        slot = lax.broadcasted_iota(jnp.int32, (1, count), 1)
        source, place = divided(slot, capacity)
        lane = lax.broadcasted_iota(jnp.int32, (LANES, 1), 0)
        weigh = jnp.where(lane == place, float(DIGIT), 0.0) + jnp.where(
            lane == place + capacity, 1.0, 0.0
        )
        line = lax.broadcasted_iota(jnp.int32, (BLOCK * EXTRA, 1), 0)
        total = jnp.zeros((strip, channels), F32)
        for at in range(0, devices, BLOCK):
            some = slice(at, at + BLOCK)
            digits = packed_ref[some, cuts * capacity :].reshape(BLOCK * EXTRA, LANES)
            values = dot(digits, weigh.astype(BF16))
            target = jnp.sum(
                jnp.where(line == source * EXTRA, values, 0.0), 0, keepdims=True
            )
            rows = [
                packed_ref[some, c * capacity : (c + 1) * capacity].reshape(count, LANES)
                for c in range(cuts)
            ]
            rows = jnp.concatenate(rows, axis=1)
            total += dot(selection(cell, target.astype(jnp.int32)), rows)
        high = total.astype(BF16)
        gathered[0] = high
        gathered[1] = (total - high.astype(F32)).astype(BF16)

    lane_head = lax.broadcasted_iota(jnp.int32, (1, GROUP), 1) // width
    same_head = selection(lax.broadcasted_iota(jnp.int32, (GROUP, 1), 0) // width, lane_head)
    scale = jnp.zeros((1, GROUP), F32)
    for h in range(heads):
        scale = jnp.where(lane_head == h, scale_ref[step * heads + h] * LOG2E, scale)
    left_half = lax.broadcasted_iota(jnp.int32, (CELLS, 2 * width), 1) < width
    blank = jnp.zeros((width, CELLS), BF16)

    high = gathered[0]
    query, keys, values = (base_ref[0, i] + dot(high, folded_ref[0, i]) for i in range(3))
    query_sum = dot((query * query).astype(BF16), same_head)
    keys_sum = dot((keys * keys).astype(BF16), same_head)
    query_n = (query * (lax.rsqrt(query_sum + cosine_eps) * scale)).astype(BF16)
    keys_n = keys * lax.rsqrt(keys_sum + cosine_eps)

    def scored(w):
        here = slice(w * CELLS, (w + 1) * CELLS)
        keys_t = keys_n[here].T.astype(BF16)
        result = []
        for h in range(heads):
            pair, side = h // 2, h % 2
            lanes = slice(2 * pair * width, 2 * (pair + 1) * width)
            picked = keys_t[h * width : (h + 1) * width]
            picked = jnp.concatenate([blank, picked] if side else [picked, blank], axis=0)
            result.append(dot(query_n[here, lanes], picked))
        return result

    def weighted(w, scores):
        here = slice(w * CELLS, (w + 1) * CELLS)
        expo = [jnp.exp2(scores[h] + bias_ref[h]).astype(BF16) for h in range(heads)]
        sums = []
        for h in range(heads):
            lanes = slice(h // 2 * 2 * width, (h // 2 + 1) * 2 * width)
            mixed = jnp.where(left_half == (h % 2 == 0), values[here, lanes], 1.0).astype(BF16)
            sums.append(dot(expo[h], mixed))
        parts = []
        for a, b in zip(sums[::2], sums[1::2]):
            norm = pltpu.roll(jnp.where(left_half, b, a), width, 1)
            parts.append(jnp.where(left_half, a, b) / norm)
        context[step, here] = jnp.concatenate(parts, axis=1).astype(BF16)

    scores = scored(0)
    for w in range(windows):
        after = scored(w + 1) if w + 1 < windows else None
        weighted(w, scores)
        scores = after

    @pl.when(step == groups - 1)
    def _():
        for copy in copies:
            copy.wait()
        pieces = 2
        size = strip // pieces
        cuts = [slice(at * size, (at + 1) * size) for at in range(pieces)]
        projs = [
            dot(jnp.concatenate([context[g, cut] for g in range(groups)], axis=1), w_out_ref[...])
            for cut in cuts
        ]
        latents = [
            ordered_ref[cut].astype(F32)
            + dot(gathered[0, cut], w_obs_ref[...])
            + dot(gathered[1, cut], w_obs_ref[...])
            for cut in cuts
        ]
        done = []
        for proj, latent in zip(projs, latents):
            center = proj - jnp.mean(proj, -1, keepdims=True)
            spread = jnp.mean(center * center, -1, keepdims=True)
            normed = center * lax.rsqrt(spread + layer_eps) * gain_ref[...]
            done.append((latent + normed).astype(BF16))
        done = jnp.concatenate(done, axis=0)
        row = lax.broadcasted_iota(jnp.int32, (1, strip), 1)
        window, level, lat, lon = window_parts(row)
        level = lax.rem(level + WL // 2, jnp.full_like(level, WL))
        half, lat = divided(lat, HALF_A)
        lon = window * WO + lon
        moved = lax.rem(lon + HALF_O, jnp.full_like(lon, lon_cells))
        place = ((half * WL + level) * HALF_A + lat) * lon_cells + moved
        edge = (level * HALF_A + lat) * HALF_O + moved
        size = WL * HALF_A * lon_cells
        for h, out_ref in enumerate((near_ref, far_ref)):
            index = lax.broadcasted_iota(jnp.int32, (size, 1), 0) + h * size
            out_ref[...] = dot(selection(index, place), done).astype(BF16)
            if h == 0 or passed:
                index = lax.broadcasted_iota(jnp.int32, (EDGE, 1), 0)
                wanted = jnp.where((moved < HALF_O) & (half == h), edge, -1)
                chosen = dot(selection(index, wanted), done).astype(BF16)
                edge_ref[h * EDGE : (h + 1) * EDGE] = chosen
        if passed:
            edge_ref[2 * EDGE :] = carried_ref[...]


def attend_strip(
    strip_at, packed, scale, gain, base, folded, bias, ordered, w_obs, w_out, lat_cells, lon_cells,
    carried=None,
):
    strip = WL * WA * lon_cells
    features = w_out.shape[0]
    groups = features // GROUP
    channels = w_obs.shape[0]
    heads = bias.shape[0] // groups
    passed = carried is not None
    whole = lambda i: (0, 0)
    once = pl.Buffered(buffer_count=1)
    there = pl.BlockSpec(memory_space=pl.ANY)
    half = (strip // 2, features)
    outs = [half, half, (3 * EDGE if passed else EDGE, features)]
    extra = [carried] if passed else []
    return pl.pallas_call(
        functools.partial(strip_kernel, strip_at, lon_cells, lat_cells, passed),
        grid=(groups,),
        in_specs=[
            pl.BlockSpec(packed.shape, lambda i: (0, 0, 0), pipeline_mode=once),
            pl.BlockSpec(memory_space=pltpu.SMEM),
            pl.BlockSpec((1, features), whole),
            pl.BlockSpec((1, 3, strip, GROUP), lambda i: (i, 0, strip_at, 0)),
            pl.BlockSpec((1, 3, channels, GROUP), lambda i: (i, 0, 0, 0)),
            pl.BlockSpec((heads, CELLS, CELLS), lambda i: (i, 0, 0)),
            there,
            there,
            there,
        ]
        + [pl.BlockSpec(part.shape, whole, pipeline_mode=once) for part in extra],
        out_specs=[pl.BlockSpec(shape, whole) for shape in outs],
        out_shape=[jax.ShapeDtypeStruct(shape, BF16) for shape in outs],
        scratch_shapes=[
            pltpu.VMEM((strip, features), BF16),
            pltpu.VMEM(w_obs.shape, BF16),
            pltpu.VMEM(w_out.shape, BF16),
            pltpu.VMEM((2, strip, channels), BF16),
            pltpu.VMEM((groups, strip, GROUP), BF16),
            pltpu.SemaphoreType.DMA((3,)),
        ],
        compiler_params=pltpu.CompilerParams(vmem_limit_bytes=32 * MIB),
        cost_estimate=pl.CostEstimate(
            flops=14 * strip * features * features,
            bytes_accessed=12 * strip * features + 8 * features * features,
            transcendentals=strip * CELLS * bias.shape[0],
        ),
    )(packed, scale, gain, base, folded, bias, ordered, w_obs, w_out, *extra)


def corner_kernel(lon_cells, block_ref, edge_ref):
    size = block_ref.shape[0]
    line, moved = divided(lax.broadcasted_iota(jnp.int32, (1, size), 1), lon_cells)
    wanted = jnp.where(moved < HALF_O, line * HALF_O + moved, -1)
    index = lax.broadcasted_iota(jnp.int32, (EDGE, 1), 0)
    edge_ref[...] = dot(selection(index, wanted), block_ref[...]).astype(BF16)


def corner(block, lon_cells):
    size, features = block.shape
    return pl.pallas_call(
        functools.partial(corner_kernel, lon_cells),
        out_shape=jax.ShapeDtypeStruct((EDGE, features), BF16),
        compiler_params=pltpu.CompilerParams(vmem_limit_bytes=16 * MIB),
        cost_estimate=pl.CostEstimate(
            flops=2 * EDGE * size * features, bytes_accessed=2 * size * features, transcendentals=0
        ),
    )(block)


def join_kernel(lon_cells, count, *refs):
    ins, out_ref = refs[:-1], refs[-1]
    size = WL * HALF_A * lon_cells
    row = lax.broadcasted_iota(jnp.int32, (size, 1), 0)
    line, moved = divided(row, lon_cells)
    edge = jnp.where(moved < HALF_O, line * HALF_O + moved, -1)
    insert = selection(edge, lax.broadcasted_iota(jnp.int32, (1, EDGE), 1))
    for at in range(count):

        @pl.when(pl.program_id(0) == at)
        def _():
            block_ref, edge_ref = ins[2 * at : 2 * at + 2]
            west = dot(insert, edge_ref[...])
            full = jnp.where(moved < HALF_O, west, block_ref[...].astype(F32)).astype(BF16)
            half = size // WL
            for l in range(WL):
                out_ref[l, 0] = full[l * half : (l + 1) * half]


def join(blocks, lon_cells):
    features = blocks[0][0].shape[-1]
    size = WL * HALF_A * lon_cells
    flat, specs = [], []
    for block, edges, at in blocks:
        flat += [block, edges]
        specs.append(pl.BlockSpec((size, features), lambda i: (0, 0)))
        specs.append(pl.BlockSpec((EDGE, features), lambda i, at=at: (at, 0)))
    return pl.pallas_call(
        functools.partial(join_kernel, lon_cells, len(blocks)),
        grid=(len(blocks),),
        in_specs=specs,
        out_specs=pl.BlockSpec((WL, 1, size // WL, features), lambda i: (0, i, 0, 0)),
        out_shape=jax.ShapeDtypeStruct((WL, len(blocks), size // WL, features), BF16),
        compiler_params=pltpu.CompilerParams(vmem_limit_bytes=16 * MIB),
        cost_estimate=pl.CostEstimate(
            flops=0, bytes_accessed=4 * len(blocks) * size * features, transcendentals=0
        ),
    )(*flat)


def body(
    latent_state,
    obs_rows,
    obs_cells,
    obs_counts,
    w_obs,
    w_qkv,
    w_out,
    logit_scale,
    pos_bias,
    out_gain,
):
    levels, lat_cells, lon_cells, features = latent_state.shape
    lat_devices = lax.axis_size("lat")
    lon_devices = lax.axis_size("lon")
    devices = lat_devices * lon_devices
    both = ("lat", "lon")
    capacity = obs_rows.shape[2] // devices
    channels = obs_rows.shape[3]

    packed = pack(
        obs_rows.reshape(devices, capacity, channels),
        obs_cells.reshape(1, devices * capacity),
        obs_counts.reshape(1, devices),
    )
    packed = lax.all_to_all(packed, both, split_axis=0, concat_axis=0, tiled=True)
    base, folded, ordered, bias = project(
        latent_state.reshape(-1, features), w_obs, w_qkv, pos_bias, lon_cells
    )
    gain = out_gain[None]

    def attend(strip_at, carried=None):
        return attend_strip(
            strip_at, packed, logit_scale, gain, base, folded, bias, ordered, w_obs, w_out,
            lat_cells, lon_cells, carried,
        )

    south = [(i, i + 1) for i in range(lat_devices - 1)]
    east = [(i, (i + 1) % lon_devices) for i in range(lon_devices)]
    low_near, low_far, low_edge = attend(1)
    first = lax.ppermute(low_far, "lat", south)
    top_near, top_far, edges = attend(0, low_edge)
    edges = lax.ppermute(edges, "lon", east)
    first_edge = lax.ppermute(corner(first, lon_cells), "lon", east)
    joined = join(
        [
            (first, first_edge, 0),
            (top_near, edges, 0),
            (top_far, edges, 1),
            (low_near, edges, 2),
        ],
        lon_cells,
    )
    return joined.reshape(levels, lat_cells, lon_cells, features)


def solution(mesh):
    in_specs = (
        P(None, "lat", "lon", None),
        P("lat", "lon", None, None),
        P("lat", "lon", None),
        P("lat", "lon", None),
        P(),
        P(),
        P(),
        P(),
        P(),
        P(),
    )
    out_specs = P(None, "lat", "lon", None)
    return jax.shard_map(body, mesh=mesh, in_specs=in_specs, out_specs=out_specs, check_vma=False)
```

```python
import functools
import math

import jax
import jax.numpy as jnp
from jax import lax
from jax.experimental import pallas as pl
from jax.experimental.pallas import tpu as pltpu
from jax.sharding import PartitionSpec as P

WL = 2
WA = 12
WO = 6
CELLS = WL * WA * WO
HALF_A = WA // 2
HALF_O = WO // 2
GROUP = 256
EXTRA = 8
BLOCK = 32
DIGIT = 32
DEAD = 255
EDGE = 48

cosine_eps = 1e-06
layer_eps = 1e-05
LOG2E = math.log2(math.e)
MIB = 1024 * 1024
LANES = 128

F32 = jnp.float32
BF16 = jnp.bfloat16


def divided(x, n):
    quotient = lax.div(x, jnp.full_like(x, n))
    return quotient, x - quotient * n


def window_parts(row):
    window, inner = divided(row, CELLS)
    level, inner = divided(inner, WA * WO)
    lat, lon = divided(inner, WO)
    return window, level, lat, lon


def dot(a, b):
    return jnp.dot(a, b, preferred_element_type=F32)


def selection(rows, columns):
    return (rows == columns).astype(F32).astype(BF16)


def pinned(x):
    return pltpu.with_memory_space_constraint(x, pltpu.HBM)


def pack_kernel(rows_ref, cells_ref, counts_ref, packed_ref):
    devices, capacity, channels = rows_ref.shape
    slots = devices * capacity
    for at in range(channels // LANES):
        part = rows_ref[:, :, at * LANES : (at + 1) * LANES]
        packed_ref[:, at * capacity : (at + 1) * capacity] = part
    cells = cells_ref[...]
    high = lax.div(cells, jnp.full_like(cells, DIGIT))
    low = cells - high * DIGIT
    slot = lax.broadcasted_iota(jnp.int32, (1, slots), 1)
    device = lax.broadcasted_iota(jnp.int32, (devices, 1), 0)
    place = lax.broadcasted_iota(jnp.int32, (slots, 1), 0)
    place = lax.rem(place, jnp.full_like(place, capacity))
    lane = lax.broadcasted_iota(jnp.int32, (1, LANES), 1)
    own = divided(slot, capacity)[0] == device
    digits = jnp.zeros((devices, LANES), F32)
    for i, digit in enumerate((high, low)):
        spread = jnp.where(own, digit.astype(F32), 0.0).astype(BF16)
        digits += dot(spread, selection(place + i * capacity, lane))
    same = device == lax.broadcasted_iota(jnp.int32, (1, devices), 1)
    count = jnp.sum(jnp.where(same, counts_ref[...].astype(F32), 0.0), -1, keepdims=True)
    dead = (lane < capacity) & (lane.astype(F32) >= count)
    digits = jnp.where(dead, float(DEAD), digits)
    packed_ref[:, channels // LANES * capacity :] = jnp.broadcast_to(
        digits[:, None, :], (devices, EXTRA, LANES)
    ).astype(BF16)


def pack(rows, cells, counts):
    devices, capacity, channels = rows.shape
    held = channels // LANES * capacity + EXTRA
    return pl.pallas_call(
        pack_kernel,
        out_shape=jax.ShapeDtypeStruct((devices, held, LANES), BF16),
        compiler_params=pltpu.CompilerParams(vmem_limit_bytes=16 * MIB),
    )(pinned(rows), pinned(cells), pinned(counts))


def project_kernel(
    lon_cells,
    latent_ref,
    w_obs_ref,
    wq_ref,
    wk_ref,
    wv_ref,
    bias_ref,
    base_ref,
    folded_ref,
    scaled_ref,
    left,
):
    rows = latent_ref.shape[0]
    strip = WL * WA * lon_cells
    strips = rows // strip
    part = WA * lon_cells

    @pl.when(pl.program_id(0) == 0)
    def _():
        row = lax.broadcasted_iota(jnp.int32, (strip, 1), 0)
        window, level, lat, lon = window_parts(row)
        source = level * part + lat * lon_cells + window * WO + lon
        perm = selection(source, lax.broadcasted_iota(jnp.int32, (1, strip), 1))
        for s in range(strips):
            cells = jnp.concatenate(
                [
                    latent_ref[l * strips * part + s * part : l * strips * part + (s + 1) * part]
                    for l in range(WL)
                ],
                axis=0,
            )
            left[s * strip : (s + 1) * strip] = dot(perm, cells).astype(BF16)
        left[rows:] = w_obs_ref[...]

    for i, w_ref in enumerate((wq_ref, wk_ref, wv_ref)):
        result = dot(left[...], w_ref[...])
        base_ref[0, i] = result[:rows]
        folded_ref[0, i] = result[rows:].astype(BF16)
    scaled_ref[...] = bias_ref[...] * LOG2E


def project(latent, w_obs, w_qkv, bias, lon_cells):
    rows, features = latent.shape
    channels = w_obs.shape[0]
    columns = w_qkv.shape[1]
    groups = features // GROUP
    heads = bias.shape[0] // groups
    whole = lambda i: (0, 0)
    once = pl.Buffered(buffer_count=1)
    some_heads = pl.BlockSpec((heads, CELLS, CELLS), lambda i: (i, 0, 0))
    return pl.pallas_call(
        functools.partial(project_kernel, lon_cells),
        grid=(groups,),
        in_specs=[
            pl.BlockSpec((rows, features), whole, pipeline_mode=once),
            pl.BlockSpec((channels, features), whole, pipeline_mode=once),
            pl.BlockSpec((features, GROUP), lambda i: (0, i)),
            pl.BlockSpec((features, GROUP), lambda i: (0, groups + i)),
            pl.BlockSpec((features, GROUP), lambda i: (0, 2 * groups + i)),
            some_heads,
        ],
        out_specs=[
            pl.BlockSpec((1, 3, rows, GROUP), lambda i: (i, 0, 0, 0)),
            pl.BlockSpec((1, 3, channels, GROUP), lambda i: (i, 0, 0, 0)),
            some_heads,
        ],
        out_shape=[
            pltpu.HBM((groups, 3, rows, GROUP), F32),
            pltpu.HBM((groups, 3, channels, GROUP), BF16),
            pltpu.HBM(bias.shape, F32),
        ],
        scratch_shapes=[pltpu.VMEM((rows + channels, features), BF16)],
        compiler_params=pltpu.CompilerParams(vmem_limit_bytes=32 * MIB),
        cost_estimate=pl.CostEstimate(
            flops=2 * (rows + channels) * features * columns,
            bytes_accessed=4 * rows * columns + 2 * features * columns + 4 * rows * features,
            transcendentals=0,
        ),
    )(pinned(latent), pinned(w_obs), *[pinned(w_qkv)] * 3, pinned(bias))


def in_output_order(target, at, window, block, lon_cells):
    for level in range(WL):
        for lat in range(WA):
            half, line = divmod(lat, HALF_A)
            row = (half * WL + (level + WL // 2) % WL) * HALF_A + line
            source = (level * WA + lat) * WO
            moved = window * WO + HALF_O
            begin = 0
            while begin < WO:
                goal = (moved + begin) % lon_cells
                count = min(WO - begin, lon_cells - goal)
                lines = slice(row * lon_cells + goal, row * lon_cells + goal + count)
                target[lines, at] = block[source + begin : source + begin + count]
                begin += count


def strip_kernel(
    strip_at,
    lon_cells,
    passed,
    packed_ref,
    scale_ref,
    gain_ref,
    base_ref,
    folded_ref,
    bias_ref,
    latent_hbm,
    w_obs_hbm,
    w_out_hbm,
    *rest,
):
    carried_ref = rest[0] if passed else None
    (
        near_ref,
        far_ref,
        edge_ref,
        latent_ref,
        w_obs_ref,
        w_out_ref,
        gathered,
        gathered_out,
        context,
        sems,
    ) = rest[passed:]
    step = pl.program_id(0)
    lat_cells = latent_hbm.shape[1]
    features = w_out_ref.shape[0]
    strip = gathered.shape[0]
    windows = strip // CELLS
    groups = features // GROUP
    heads = bias_ref.shape[0]
    width = GROUP // heads
    devices, held, _ = packed_ref.shape
    channels = w_obs_ref.shape[0]
    cuts = channels // LANES
    capacity = (held - EXTRA) // cuts
    copies = [
        pltpu.make_async_copy(
            latent_hbm.at[:, pl.ds(strip_at * WA, WA)], latent_ref, sems.at[0]
        ),
        pltpu.make_async_copy(w_obs_hbm, w_obs_ref, sems.at[1]),
        pltpu.make_async_copy(w_out_hbm, w_out_ref, sems.at[2]),
    ]

    @pl.when(step == 0)
    def _():
        for copy in copies:
            copy.start()
        row = lax.broadcasted_iota(jnp.int32, (strip, 1), 0)
        window, level, lat, lon = window_parts(row)
        cell = (level * lat_cells + strip_at * WA + lat) * lon_cells + window * WO + lon
        count = BLOCK * capacity
        slot = lax.broadcasted_iota(jnp.int32, (1, count), 1)
        source, place = divided(slot, capacity)
        lane = lax.broadcasted_iota(jnp.int32, (LANES, 1), 0)
        weigh = jnp.where(lane == place, float(DIGIT), 0.0) + jnp.where(
            lane == place + capacity, 1.0, 0.0
        )
        line = lax.broadcasted_iota(jnp.int32, (BLOCK * EXTRA, 1), 0)
        total = jnp.zeros((strip, channels), F32)
        for at in range(0, devices, BLOCK):
            some = slice(at, at + BLOCK)
            digits = packed_ref[some, cuts * capacity :].reshape(BLOCK * EXTRA, LANES)
            values = dot(digits, weigh.astype(BF16))
            target = jnp.sum(
                jnp.where(line == source * EXTRA, values, 0.0), 0, keepdims=True
            )
            rows = [
                packed_ref[some, c * capacity : (c + 1) * capacity].reshape(count, LANES)
                for c in range(cuts)
            ]
            rows = jnp.concatenate(rows, axis=1)
            total += dot(selection(cell, target.astype(jnp.int32)), rows)
        gathered[...] = total.astype(BF16)
        for w in range(windows):
            block = total[w * CELLS : (w + 1) * CELLS]
            in_output_order(gathered_out, slice(None), w, block, lon_cells)

    lane_head = lax.broadcasted_iota(jnp.int32, (1, GROUP), 1) // width
    same_head = selection(lax.broadcasted_iota(jnp.int32, (GROUP, 1), 0) // width, lane_head)
    scale = jnp.zeros((1, GROUP), F32)
    for h in range(heads):
        scale = jnp.where(lane_head == h, scale_ref[step * heads + h] * LOG2E, scale)
    left_half = lax.broadcasted_iota(jnp.int32, (CELLS, 2 * width), 1) < width
    blank = jnp.zeros((width, CELLS), BF16)

    high = gathered[...]
    query, keys, values = (base_ref[0, i] + dot(high, folded_ref[0, i]) for i in range(3))
    query_sum = dot((query * query).astype(BF16), same_head)
    query_n = (query * (lax.rsqrt(query_sum + cosine_eps) * scale)).astype(BF16)

    def scored(w):
        here = slice(w * CELLS, (w + 1) * CELLS)
        keys_t = keys[here].T
        result = []
        for h in range(heads):
            pair, side = h // 2, h % 2
            lanes = slice(2 * pair * width, 2 * (pair + 1) * width)
            own = keys_t[h * width : (h + 1) * width]
            own = own * lax.rsqrt(jnp.sum(own * own, 0, keepdims=True) + cosine_eps)
            own = own.astype(BF16)
            own = jnp.concatenate([blank, own] if side else [own, blank], axis=0)
            result.append(dot(query_n[here, lanes], own))
        return result

    def weighted(w, scores):
        here = slice(w * CELLS, (w + 1) * CELLS)
        expo = [jnp.exp2(scores[h] + bias_ref[h]).astype(BF16) for h in range(heads)]
        sums = []
        for h in range(heads):
            lanes = slice(h // 2 * 2 * width, (h // 2 + 1) * 2 * width)
            mixed = jnp.where(left_half == (h % 2 == 0), values[here, lanes], 1.0).astype(BF16)
            sums.append(dot(expo[h], mixed))
        parts = []
        for a, b in zip(sums[::2], sums[1::2]):
            norm = pltpu.roll(jnp.where(left_half, b, a), width, 1)
            guess = pl.reciprocal(norm, approx=True)
            parts.append(jnp.where(left_half, a, b) * (guess * (2.0 - norm * guess)))
        in_output_order(
            context.at[step], slice(None), w, jnp.concatenate(parts, axis=1), lon_cells
        )

    scores = scored(0)
    for w in range(windows):
        after = scored(w + 1) if w + 1 < windows else None
        weighted(w, scores)
        scores = after

    @pl.when(step == groups - 1)
    def _():
        for copy in copies:
            copy.wait()
        size = strip // 2
        line, moved = divided(lax.broadcasted_iota(jnp.int32, (1, size), 1), lon_cells)
        wanted = jnp.where(moved < HALF_O, line * HALF_O + moved, -1)
        pick = selection(lax.broadcasted_iota(jnp.int32, (EDGE, 1), 0), wanted)
        halves = [slice(h * size, (h + 1) * size) for h in range(2)]
        projs = [
            dot(
                jnp.concatenate([context[g, here].astype(BF16) for g in range(groups)], axis=1),
                w_out_ref[...],
            )
            for here in halves
        ]
        added = [dot(gathered_out[here].astype(BF16), w_obs_ref[...]) for here in halves]
        for h, out_ref in enumerate((near_ref, far_ref)):
            runs = []
            for l in range(WL):
                own = latent_ref[(l - WL // 2) % WL, h * HALF_A : (h + 1) * HALF_A].astype(F32)
                own = jnp.concatenate(
                    [own[:, lon_cells - HALF_O :], own[:, : lon_cells - HALF_O]], axis=1
                )
                runs.append(own.reshape(HALF_A * lon_cells, features))
            latent = jnp.concatenate(runs, axis=0) + added[h]
            proj = projs[h]
            center = proj - jnp.mean(proj, -1, keepdims=True)
            spread = jnp.mean(center * center, -1, keepdims=True)
            normed = center * lax.rsqrt(spread + layer_eps) * gain_ref[...]
            done = (latent + normed).astype(BF16)
            out_ref[...] = done
            if h == 0 or passed:
                edge_ref[h * EDGE : (h + 1) * EDGE] = dot(pick, done).astype(BF16)
        if passed:
            edge_ref[2 * EDGE :] = carried_ref[...]


def attend_strip(
    strip_at, packed, scale, gain, base, folded, bias, latent, w_obs, w_out, carried=None
):
    levels, lat_cells, lon_cells, features = latent.shape
    strip = WL * WA * lon_cells
    groups = features // GROUP
    channels = w_obs.shape[0]
    heads = bias.shape[0] // groups
    passed = carried is not None
    whole = lambda i: (0, 0)
    once = pl.Buffered(buffer_count=1)
    there = pl.BlockSpec(memory_space=pl.ANY)
    half = (strip // 2, features)
    outs = [half, half, (3 * EDGE if passed else EDGE, features)]
    extra = [carried] if passed else []
    return pl.pallas_call(
        functools.partial(strip_kernel, strip_at, lon_cells, passed),
        grid=(groups,),
        in_specs=[
            pl.BlockSpec(packed.shape, lambda i: (0, 0, 0), pipeline_mode=once),
            pl.BlockSpec(memory_space=pltpu.SMEM),
            pl.BlockSpec((1, features), whole),
            pl.BlockSpec((1, 3, strip, GROUP), lambda i: (i, 0, strip_at, 0)),
            pl.BlockSpec((1, 3, channels, GROUP), lambda i: (i, 0, 0, 0)),
            pl.BlockSpec((heads, CELLS, CELLS), lambda i: (i, 0, 0)),
            there,
            there,
            there,
        ]
        + [pl.BlockSpec(part.shape, whole, pipeline_mode=once) for part in extra],
        out_specs=[pl.BlockSpec(shape, whole) for shape in outs],
        out_shape=[jax.ShapeDtypeStruct(shape, BF16) for shape in outs],
        scratch_shapes=[
            pltpu.VMEM((levels, WA, lon_cells, features), BF16),
            pltpu.VMEM(w_obs.shape, BF16),
            pltpu.VMEM(w_out.shape, BF16),
            pltpu.VMEM((strip, channels), BF16),
            pltpu.VMEM((strip, channels), F32),
            pltpu.VMEM((groups, strip, GROUP), F32),
            pltpu.SemaphoreType.DMA((3,)),
        ],
        compiler_params=pltpu.CompilerParams(vmem_limit_bytes=40 * MIB),
        cost_estimate=pl.CostEstimate(
            flops=14 * strip * features * features,
            bytes_accessed=12 * strip * features + 8 * features * features,
            transcendentals=strip * CELLS * bias.shape[0],
        ),
    )(
        packed,
        scale,
        pinned(gain),
        pinned(base),
        pinned(folded),
        pinned(bias),
        pinned(latent),
        pinned(w_obs),
        pinned(w_out),
        *extra,
    )


def corner_kernel(lon_cells, block_ref, edge_ref):
    size = block_ref.shape[0]
    line, moved = divided(lax.broadcasted_iota(jnp.int32, (1, size), 1), lon_cells)
    wanted = jnp.where(moved < HALF_O, line * HALF_O + moved, -1)
    index = lax.broadcasted_iota(jnp.int32, (EDGE, 1), 0)
    edge_ref[...] = dot(selection(index, wanted), block_ref[...]).astype(BF16)


def corner(block, lon_cells):
    size, features = block.shape
    return pl.pallas_call(
        functools.partial(corner_kernel, lon_cells),
        out_shape=jax.ShapeDtypeStruct((EDGE, features), BF16),
        compiler_params=pltpu.CompilerParams(vmem_limit_bytes=16 * MIB),
        cost_estimate=pl.CostEstimate(
            flops=2 * EDGE * size * features, bytes_accessed=2 * size * features, transcendentals=0
        ),
    )(block)


def join_kernel(lon_cells, count, *refs):
    ins, out_ref = refs[:-1], refs[-1]
    size = WL * HALF_A * lon_cells
    row = lax.broadcasted_iota(jnp.int32, (size, 1), 0)
    line, moved = divided(row, lon_cells)
    edge = jnp.where(moved < HALF_O, line * HALF_O + moved, -1)
    insert = selection(edge, lax.broadcasted_iota(jnp.int32, (1, EDGE), 1))
    for at in range(count):

        @pl.when(pl.program_id(0) == at)
        def _():
            block_ref, edge_ref = ins[2 * at : 2 * at + 2]
            west = dot(insert, edge_ref[...])
            full = jnp.where(moved < HALF_O, west, block_ref[...].astype(F32)).astype(BF16)
            half = size // WL
            for l in range(WL):
                out_ref[l, 0] = full[l * half : (l + 1) * half]


def join(blocks, lon_cells):
    features = blocks[0][0].shape[-1]
    size = WL * HALF_A * lon_cells
    flat, specs = [], []
    for block, edges, at in blocks:
        flat += [block, edges]
        specs.append(pl.BlockSpec((size, features), lambda i: (0, 0)))
        specs.append(pl.BlockSpec((EDGE, features), lambda i, at=at: (at, 0)))
    return pl.pallas_call(
        functools.partial(join_kernel, lon_cells, len(blocks)),
        grid=(len(blocks),),
        in_specs=specs,
        out_specs=pl.BlockSpec((WL, 1, size // WL, features), lambda i: (0, i, 0, 0)),
        out_shape=jax.ShapeDtypeStruct((WL, len(blocks), size // WL, features), BF16),
        compiler_params=pltpu.CompilerParams(vmem_limit_bytes=16 * MIB),
        cost_estimate=pl.CostEstimate(
            flops=0, bytes_accessed=4 * len(blocks) * size * features, transcendentals=0
        ),
    )(*flat)


def body(
    latent_state,
    obs_rows,
    obs_cells,
    obs_counts,
    w_obs,
    w_qkv,
    w_out,
    logit_scale,
    pos_bias,
    out_gain,
):
    levels, lat_cells, lon_cells, features = latent_state.shape
    lat_devices = lax.axis_size("lat")
    lon_devices = lax.axis_size("lon")
    devices = lat_devices * lon_devices
    both = ("lat", "lon")
    capacity = obs_rows.shape[2] // devices
    channels = obs_rows.shape[3]

    packed = pack(
        obs_rows.reshape(devices, capacity, channels),
        obs_cells.reshape(1, devices * capacity),
        obs_counts.reshape(1, devices),
    )
    packed = lax.all_to_all(packed, both, split_axis=0, concat_axis=0, tiled=True)
    base, folded, bias = project(
        latent_state.reshape(-1, features), w_obs, w_qkv, pos_bias, lon_cells
    )
    gain = out_gain[None]

    def attend(strip_at, carried=None):
        return attend_strip(
            strip_at, packed, logit_scale, gain, base, folded, bias, latent_state, w_obs, w_out, carried
        )

    south = [(i, i + 1) for i in range(lat_devices - 1)]
    east = [(i, (i + 1) % lon_devices) for i in range(lon_devices)]
    low_near, low_far, low_edge = attend(1)
    first = lax.ppermute(low_far, "lat", south)
    top_near, top_far, edges = attend(0, low_edge)
    edges = lax.ppermute(edges, "lon", east)
    first_edge = lax.ppermute(corner(first, lon_cells), "lon", east)
    joined = join(
        [
            (first, first_edge, 0),
            (top_near, edges, 0),
            (top_far, edges, 1),
            (low_near, edges, 2),
        ],
        lon_cells,
    )
    return joined.reshape(levels, lat_cells, lon_cells, features)


def solution(mesh):
    in_specs = (
        P(None, "lat", "lon", None),
        P("lat", "lon", None, None),
        P("lat", "lon", None),
        P("lat", "lon", None),
        P(),
        P(),
        P(),
        P(),
        P(),
        P(),
    )
    out_specs = P(None, "lat", "lon", None)
    return jax.shard_map(body, mesh=mesh, in_specs=in_specs, out_specs=out_specs, check_vma=False)
```

```python
import functools
import math

import jax
import jax.numpy as jnp
from jax import lax
from jax.experimental import pallas as pl
from jax.experimental.pallas import tpu as pltpu
from jax.sharding import PartitionSpec as P

WL = 2
WA = 12
WO = 6
CELLS = WL * WA * WO
HALF_A = WA // 2
HALF_O = WO // 2
GROUP = 256
EXTRA = 8
BLOCK = 32
DIGIT = 32
DEAD = 255
EDGE = 48

cosine_eps = 1e-06
layer_eps = 1e-05
LOG2E = math.log2(math.e)
MIB = 1024 * 1024
LANES = 128

F32 = jnp.float32
BF16 = jnp.bfloat16


def divided(x, n):
    quotient = lax.div(x, jnp.full_like(x, n))
    return quotient, x - quotient * n


def window_parts(row):
    window, inner = divided(row, CELLS)
    level, inner = divided(inner, WA * WO)
    lat, lon = divided(inner, WO)
    return window, level, lat, lon


def dot(a, b):
    return jnp.dot(a, b, preferred_element_type=F32)


def selection(rows, columns):
    return (rows == columns).astype(F32).astype(BF16)


def pinned(x):
    return pltpu.with_memory_space_constraint(x, pltpu.HBM)


def pack_kernel(rows_ref, cells_ref, counts_ref, packed_ref):
    devices, capacity, channels = rows_ref.shape
    slots = devices * capacity
    for at in range(channels // LANES):
        part = rows_ref[:, :, at * LANES : (at + 1) * LANES]
        packed_ref[:, at * capacity : (at + 1) * capacity] = part
    cells = cells_ref[...]
    high = lax.div(cells, jnp.full_like(cells, DIGIT))
    low = cells - high * DIGIT
    slot = lax.broadcasted_iota(jnp.int32, (1, slots), 1)
    device = lax.broadcasted_iota(jnp.int32, (devices, 1), 0)
    place = lax.broadcasted_iota(jnp.int32, (slots, 1), 0)
    place = lax.rem(place, jnp.full_like(place, capacity))
    lane = lax.broadcasted_iota(jnp.int32, (1, LANES), 1)
    own = divided(slot, capacity)[0] == device
    digits = jnp.zeros((devices, LANES), F32)
    for i, digit in enumerate((high, low)):
        spread = jnp.where(own, digit.astype(F32), 0.0).astype(BF16)
        digits += dot(spread, selection(place + i * capacity, lane))
    same = device == lax.broadcasted_iota(jnp.int32, (1, devices), 1)
    count = jnp.sum(jnp.where(same, counts_ref[...].astype(F32), 0.0), -1, keepdims=True)
    dead = (lane < capacity) & (lane.astype(F32) >= count)
    digits = jnp.where(dead, float(DEAD), digits)
    packed_ref[:, channels // LANES * capacity :] = jnp.broadcast_to(
        digits[:, None, :], (devices, EXTRA, LANES)
    ).astype(BF16)


def pack(rows, cells, counts):
    devices, capacity, channels = rows.shape
    held = channels // LANES * capacity + EXTRA
    return pl.pallas_call(
        pack_kernel,
        out_shape=jax.ShapeDtypeStruct((devices, held, LANES), BF16),
        compiler_params=pltpu.CompilerParams(vmem_limit_bytes=16 * MIB),
    )(pinned(rows), pinned(cells), pinned(counts))


def project_kernel(
    lon_cells, latent_hbm, w_obs_hbm, w_hbm, bias_hbm, base_ref, folded_ref, scaled_ref, latent_ref,
    w_ref, left, sems,
):
    rows, features = latent_ref.shape
    part = WA * lon_cells
    strip = WL * part
    strips = rows // strip
    groups = features // GROUP
    windows = lon_cells // WO
    first, second = 8 * lon_cells, (WA - 8) * lon_cells

    def columns(j):
        at = lax.rem(j, 3) * groups + lax.div(j, 3)
        return pl.ds(pl.multiple_of(at * GROUP, GROUP), GROUP)

    def fetched(j):
        return pltpu.make_async_copy(w_hbm.at[:, columns(j)], w_ref.at[j], sems.at[j])

    copies = []
    for s in range(strips):
        for l in range(WL):
            lines = pl.ds((l * strips + s) * part, part)
            at = 3 * groups + len(copies)
            copies.append(
                pltpu.make_async_copy(latent_hbm.at[lines], latent_ref.at[lines], sems.at[at])
            )
    at = 3 * groups + len(copies)
    copies.append(pltpu.make_async_copy(w_obs_hbm, left.at[pl.ds(rows, w_obs_hbm.shape[0])], sems.at[at]))
    copies.append(pltpu.make_async_copy(bias_hbm, scaled_ref, sems.at[at + 1]))
    for copy in copies[:-1]:
        copy.start()
    for j in range(3 * groups):
        fetched(j).start()
    copies[-1].start()

    perms = []
    for lines in (first, second):
        run = lines // windows
        row = lax.broadcasted_iota(jnp.int32, (lines, 1), 0)
        window, inner = divided(row, run)
        lat, lon = divided(inner, WO)
        source = lat * lon_cells + window * WO + lon
        perms.append(selection(source, lax.broadcasted_iota(jnp.int32, (1, lines), 1)))
    for s in range(strips):
        moved = []
        for l in range(WL):
            copies[s * WL + l].wait()
            begin = (l * strips + s) * part
            moved.append(dot(perms[0], latent_ref[begin : begin + first]))
            moved.append(dot(perms[1], latent_ref[begin + first : begin + part]))
        for w in range(windows):
            runs = []
            for piece in moved:
                run = piece.shape[0] // windows
                runs.append(piece[w * run : (w + 1) * run])
            at = s * strip + w * CELLS
            left[at : at + CELLS] = jnp.concatenate(runs, axis=0).astype(BF16)
    copies[-2].wait()

    def multiply(j, carry):
        fetched(j).wait()
        result = dot(left[...], w_ref[j])
        base_ref[j] = result[:rows]
        folded_ref[j] = result[rows:].astype(BF16)
        return carry

    lax.fori_loop(0, 3 * groups, multiply, 0)
    copies[-1].wait()
    scaled_ref[...] = scaled_ref[...] * LOG2E


def project(latent, w_obs, w_qkv, bias, lon_cells):
    rows, features = latent.shape
    channels = w_obs.shape[0]
    columns = w_qkv.shape[1]
    blocks = columns // GROUP
    strips = rows // (WL * WA * lon_cells)
    there = pl.BlockSpec(memory_space=pl.ANY)
    here = pl.BlockSpec(memory_space=pltpu.VMEM)
    return pl.pallas_call(
        functools.partial(project_kernel, lon_cells),
        in_specs=[there] * 4,
        out_specs=[here] * 3,
        out_shape=[
            pltpu.VMEM((blocks, rows, GROUP), F32),
            pltpu.VMEM((blocks, channels, GROUP), BF16),
            pltpu.VMEM(bias.shape, F32),
        ],
        scratch_shapes=[
            pltpu.VMEM((rows, features), BF16),
            pltpu.VMEM((blocks, features, GROUP), BF16),
            pltpu.VMEM((rows + channels, features), BF16),
            pltpu.SemaphoreType.DMA((blocks + WL * strips + 2,)),
        ],
        compiler_params=pltpu.CompilerParams(vmem_limit_bytes=24 * MIB),
        cost_estimate=pl.CostEstimate(
            flops=2 * (rows + channels) * features * columns,
            bytes_accessed=4 * rows * columns + 2 * features * columns + 4 * rows * features,
            transcendentals=0,
        ),
    )(pinned(latent), pinned(w_obs), pinned(w_qkv), pinned(bias))


def in_output_order(target, at, window, block, lon_cells):
    for level in range(WL):
        for lat in range(WA):
            half, line = divmod(lat, HALF_A)
            row = (half * WL + (level + WL // 2) % WL) * HALF_A + line
            source = (level * WA + lat) * WO
            moved = window * WO + HALF_O
            begin = 0
            while begin < WO:
                goal = (moved + begin) % lon_cells
                count = min(WO - begin, lon_cells - goal)
                lines = slice(row * lon_cells + goal, row * lon_cells + goal + count)
                target[lines, at] = block[source + begin : source + begin + count]
                begin += count


def strip_kernel(
    strip_at,
    lon_cells,
    passed,
    packed_ref,
    scale_ref,
    gain_ref,
    base_ref,
    folded_ref,
    bias_ref,
    latent_hbm,
    w_obs_hbm,
    w_out_hbm,
    *rest,
):
    carried_ref = rest[0] if passed else None
    (
        near_ref,
        far_ref,
        edge_ref,
        latent_ref,
        w_obs_ref,
        w_out_ref,
        gathered,
        gathered_out,
        context,
        sems,
    ) = rest[passed:]
    lat_cells = latent_hbm.shape[1]
    features = w_out_ref.shape[0]
    strip = gathered.shape[0]
    windows = strip // CELLS
    groups = features // GROUP
    heads = bias_ref.shape[0] // groups
    width = GROUP // heads
    devices, held, _ = packed_ref.shape
    channels = w_obs_ref.shape[0]
    cuts = channels // LANES
    capacity = (held - EXTRA) // cuts
    copies = [
        pltpu.make_async_copy(
            latent_hbm.at[:, pl.ds(strip_at * WA, WA)], latent_ref, sems.at[0]
        ),
        pltpu.make_async_copy(w_obs_hbm, w_obs_ref, sems.at[1]),
        pltpu.make_async_copy(w_out_hbm, w_out_ref, sems.at[2]),
    ]

    for copy in copies:
        copy.start()
    row = lax.broadcasted_iota(jnp.int32, (strip, 1), 0)
    window, level, lat, lon = window_parts(row)
    cell = (level * lat_cells + strip_at * WA + lat) * lon_cells + window * WO + lon
    count = BLOCK * capacity
    slot = lax.broadcasted_iota(jnp.int32, (1, count), 1)
    source, place = divided(slot, capacity)
    lane = lax.broadcasted_iota(jnp.int32, (LANES, 1), 0)
    weigh = jnp.where(lane == place, float(DIGIT), 0.0) + jnp.where(
        lane == place + capacity, 1.0, 0.0
    )
    line = lax.broadcasted_iota(jnp.int32, (BLOCK * EXTRA, 1), 0)
    total = jnp.zeros((strip, channels), F32)
    for at in range(0, devices, BLOCK):
        some = slice(at, at + BLOCK)
        digits = packed_ref[some, cuts * capacity :].reshape(BLOCK * EXTRA, LANES)
        values = dot(digits, weigh.astype(BF16))
        target = jnp.sum(
            jnp.where(line == source * EXTRA, values, 0.0), 0, keepdims=True
        )
        rows = [
            packed_ref[some, c * capacity : (c + 1) * capacity].reshape(count, LANES)
            for c in range(cuts)
        ]
        rows = jnp.concatenate(rows, axis=1)
        total += dot(selection(cell, target.astype(jnp.int32)), rows)
    gathered[...] = total.astype(BF16)
    for w in range(windows):
        block = total[w * CELLS : (w + 1) * CELLS]
        in_output_order(gathered_out, slice(None), w, block, lon_cells)

    lane_head = lax.broadcasted_iota(jnp.int32, (1, GROUP), 1) // width
    same_head = selection(lax.broadcasted_iota(jnp.int32, (GROUP, 1), 0) // width, lane_head)
    left_half = lax.broadcasted_iota(jnp.int32, (CELLS, 2 * width), 1) < width
    blank = jnp.zeros((width, CELLS), BF16)

    mine = slice(strip_at * strip, (strip_at + 1) * strip)

    def group(step, carry):
        scale = jnp.zeros((1, GROUP), F32)
        for h in range(heads):
            scale = jnp.where(lane_head == h, scale_ref[step * heads + h] * LOG2E, scale)
        high = gathered[...]
        query, keys, values = (
                base_ref[3 * step + i, mine] + dot(high, folded_ref[3 * step + i]) for i in range(3)
            )
        query_sum = dot((query * query).astype(BF16), same_head)
        query_n = (query * (lax.rsqrt(query_sum + cosine_eps) * scale)).astype(BF16)

        def scored(w):
            here = slice(w * CELLS, (w + 1) * CELLS)
            keys_t = keys[here].T
            result = []
            for h in range(heads):
                pair, side = h // 2, h % 2
                lanes = slice(2 * pair * width, 2 * (pair + 1) * width)
                own = keys_t[h * width : (h + 1) * width]
                own = own * lax.rsqrt(jnp.sum(own * own, 0, keepdims=True) + cosine_eps)
                own = own.astype(BF16)
                own = jnp.concatenate([blank, own] if side else [own, blank], axis=0)
                result.append(dot(query_n[here, lanes], own))
            return result

        def weighted(w, scores):
            here = slice(w * CELLS, (w + 1) * CELLS)
            expo = [jnp.exp2(scores[h] + bias_ref[step * heads + h]).astype(BF16) for h in range(heads)]
            sums = []
            for h in range(heads):
                lanes = slice(h // 2 * 2 * width, (h // 2 + 1) * 2 * width)
                mixed = jnp.where(left_half == (h % 2 == 0), values[here, lanes], 1.0).astype(BF16)
                sums.append(dot(expo[h], mixed))
            parts = []
            for a, b in zip(sums[::2], sums[1::2]):
                norm = pltpu.roll(jnp.where(left_half, b, a), width, 1)
                guess = pl.reciprocal(norm, approx=True)
                parts.append(jnp.where(left_half, a, b) * (guess * (2.0 - norm * guess)))
            in_output_order(
                context.at[step], slice(None), w, jnp.concatenate(parts, axis=1), lon_cells
            )

        scores = scored(0)
        for w in range(windows):
            after = scored(w + 1) if w + 1 < windows else None
            weighted(w, scores)
            scores = after
        return carry

    lax.fori_loop(0, groups, group, 0)

    for copy in copies:
        copy.wait()
    size = strip // 2
    line, moved = divided(lax.broadcasted_iota(jnp.int32, (1, size), 1), lon_cells)
    wanted = jnp.where(moved < HALF_O, line * HALF_O + moved, -1)
    pick = selection(lax.broadcasted_iota(jnp.int32, (EDGE, 1), 0), wanted)
    halves = [slice(h * size, (h + 1) * size) for h in range(2)]
    projs = [
        dot(
            jnp.concatenate([context[g, here].astype(BF16) for g in range(groups)], axis=1),
            w_out_ref[...],
        )
        for here in halves
    ]
    added = [dot(gathered_out[here].astype(BF16), w_obs_ref[...]) for here in halves]
    for h, out_ref in enumerate((near_ref, far_ref)):
        runs = []
        for l in range(WL):
            own = latent_ref[(l - WL // 2) % WL, h * HALF_A : (h + 1) * HALF_A].astype(F32)
            own = jnp.concatenate(
                [own[:, lon_cells - HALF_O :], own[:, : lon_cells - HALF_O]], axis=1
            )
            runs.append(own.reshape(HALF_A * lon_cells, features))
        latent = jnp.concatenate(runs, axis=0) + added[h]
        proj = projs[h]
        center = proj - jnp.mean(proj, -1, keepdims=True)
        spread = jnp.mean(center * center, -1, keepdims=True)
        normed = center * lax.rsqrt(spread + layer_eps) * gain_ref[...]
        done = (latent + normed).astype(BF16)
        out_ref[...] = done
        if h == 0 or passed:
            edge_ref[h * EDGE : (h + 1) * EDGE] = dot(pick, done).astype(BF16)
    if passed:
        edge_ref[2 * EDGE :] = carried_ref[...]


def attend_strip(
    strip_at, packed, scale, gain, base, folded, bias, latent, w_obs, w_out, carried=None
):
    levels, lat_cells, lon_cells, features = latent.shape
    strip = WL * WA * lon_cells
    groups = features // GROUP
    channels = w_obs.shape[0]
    heads = bias.shape[0] // groups
    passed = carried is not None
    there = pl.BlockSpec(memory_space=pl.ANY)
    here = pl.BlockSpec(memory_space=pltpu.VMEM)
    half = (strip // 2, features)
    outs = [half, half, (3 * EDGE if passed else EDGE, features)]
    extra = [carried] if passed else []
    return pl.pallas_call(
        functools.partial(strip_kernel, strip_at, lon_cells, passed),
        in_specs=[here, pl.BlockSpec(memory_space=pltpu.SMEM)]
        + [here] * 4
        + [there] * 3
        + [here] * len(extra),
        out_specs=[here] * 3,
        out_shape=[jax.ShapeDtypeStruct(shape, BF16) for shape in outs],
        scratch_shapes=[
            pltpu.VMEM((levels, WA, lon_cells, features), BF16),
            pltpu.VMEM(w_obs.shape, BF16),
            pltpu.VMEM(w_out.shape, BF16),
            pltpu.VMEM((strip, channels), BF16),
            pltpu.VMEM((strip, channels), F32),
            pltpu.VMEM((groups, strip, GROUP), F32),
            pltpu.SemaphoreType.DMA((3,)),
        ],
        compiler_params=pltpu.CompilerParams(vmem_limit_bytes=24 * MIB),
        cost_estimate=pl.CostEstimate(
            flops=14 * strip * features * features,
            bytes_accessed=12 * strip * features + 8 * features * features,
            transcendentals=strip * CELLS * bias.shape[0],
        ),
    )(
        packed,
        scale,
        gain,
        base,
        folded,
        bias,
        pinned(latent),
        pinned(w_obs),
        pinned(w_out),
        *extra,
    )


def corner_kernel(lon_cells, block_ref, edge_ref):
    size = block_ref.shape[0]
    line, moved = divided(lax.broadcasted_iota(jnp.int32, (1, size), 1), lon_cells)
    wanted = jnp.where(moved < HALF_O, line * HALF_O + moved, -1)
    index = lax.broadcasted_iota(jnp.int32, (EDGE, 1), 0)
    edge_ref[...] = dot(selection(index, wanted), block_ref[...]).astype(BF16)


def corner(block, lon_cells):
    size, features = block.shape
    return pl.pallas_call(
        functools.partial(corner_kernel, lon_cells),
        out_shape=jax.ShapeDtypeStruct((EDGE, features), BF16),
        compiler_params=pltpu.CompilerParams(vmem_limit_bytes=16 * MIB),
        cost_estimate=pl.CostEstimate(
            flops=2 * EDGE * size * features, bytes_accessed=2 * size * features, transcendentals=0
        ),
    )(block)


def join_kernel(lon_cells, count, *refs):
    ins, (out_hbm, blocks, sems) = refs[:-3], refs[-3:]
    size = WL * HALF_A * lon_cells
    half = size // WL
    row = lax.broadcasted_iota(jnp.int32, (size, 1), 0)
    line, moved = divided(row, lon_cells)
    edge = jnp.where(moved < HALF_O, line * HALF_O + moved, -1)
    insert = selection(edge, lax.broadcasted_iota(jnp.int32, (1, EDGE), 1))
    copies = []
    for at in range(count):
        block_ref, edge_ref, edge_at = ins[2 * at], ins[2 * at + 1], (0, 0, 1, 2)[at]
        west = dot(insert, edge_ref[edge_at * EDGE : (edge_at + 1) * EDGE])
        full = jnp.where(moved < HALF_O, west, block_ref[...].astype(F32)).astype(BF16)
        for l in range(WL):
            blocks[at, l] = full[l * half : (l + 1) * half]
        copies.append(pltpu.make_async_copy(blocks.at[at], out_hbm.at[:, at], sems.at[at]))
        copies[-1].start()
    for copy in copies:
        copy.wait()


def join(blocks, lon_cells):
    features = blocks[0][0].shape[-1]
    size = WL * HALF_A * lon_cells
    flat = [part for block in blocks for part in block]
    return pl.pallas_call(
        functools.partial(join_kernel, lon_cells, len(blocks)),
        in_specs=[pl.BlockSpec(memory_space=pltpu.VMEM)] * len(flat),
        out_specs=pl.BlockSpec(memory_space=pl.ANY),
        out_shape=jax.ShapeDtypeStruct((WL, len(blocks), size // WL, features), BF16),
        scratch_shapes=[
            pltpu.VMEM((len(blocks), WL, size // WL, features), BF16),
            pltpu.SemaphoreType.DMA((len(blocks),)),
        ],
        compiler_params=pltpu.CompilerParams(vmem_limit_bytes=16 * MIB),
        cost_estimate=pl.CostEstimate(
            flops=0, bytes_accessed=4 * len(blocks) * size * features, transcendentals=0
        ),
    )(*flat)


def body(
    latent_state,
    obs_rows,
    obs_cells,
    obs_counts,
    w_obs,
    w_qkv,
    w_out,
    logit_scale,
    pos_bias,
    out_gain,
):
    levels, lat_cells, lon_cells, features = latent_state.shape
    lat_devices = lax.axis_size("lat")
    lon_devices = lax.axis_size("lon")
    devices = lat_devices * lon_devices
    both = ("lat", "lon")
    capacity = obs_rows.shape[2] // devices
    channels = obs_rows.shape[3]

    packed = pack(
        obs_rows.reshape(devices, capacity, channels),
        obs_cells.reshape(1, devices * capacity),
        obs_counts.reshape(1, devices),
    )
    packed = lax.all_to_all(packed, both, split_axis=0, concat_axis=0, tiled=True)
    base, folded, bias = project(
        latent_state.reshape(-1, features), w_obs, w_qkv, pos_bias, lon_cells
    )
    gain = out_gain[None]

    def attend(strip_at, carried=None):
        return attend_strip(
            strip_at, packed, logit_scale, gain, base, folded, bias, latent_state, w_obs, w_out, carried
        )

    south = [(i, i + 1) for i in range(lat_devices - 1)]
    east = [(i, (i + 1) % lon_devices) for i in range(lon_devices)]
    low_near, low_far, low_edge = attend(1)
    first = lax.ppermute(low_far, "lat", south)
    top_near, top_far, edges = attend(0, low_edge)
    edges = lax.ppermute(edges, "lon", east)
    first_edge = lax.ppermute(corner(first, lon_cells), "lon", east)
    joined = join(
        [
            (first, first_edge),
            (top_near, edges),
            (top_far, edges),
            (low_near, edges),
        ],
        lon_cells,
    )
    return joined.reshape(levels, lat_cells, lon_cells, features)


def solution(mesh):
    in_specs = (
        P(None, "lat", "lon", None),
        P("lat", "lon", None, None),
        P("lat", "lon", None),
        P("lat", "lon", None),
        P(),
        P(),
        P(),
        P(),
        P(),
        P(),
    )
    out_specs = P(None, "lat", "lon", None)
    return jax.shard_map(body, mesh=mesh, in_specs=in_specs, out_specs=out_specs, check_vma=False)
```

```python
import functools
import math

import jax
import jax.numpy as jnp
from jax import lax
from jax.experimental import pallas as pl
from jax.experimental.pallas import tpu as pltpu
from jax.sharding import PartitionSpec as P

WL = 2
WA = 12
WO = 6
CELLS = WL * WA * WO
HALF_A = WA // 2
HALF_O = WO // 2
GROUP = 256
EXTRA = 8
BLOCK = 32
DIGIT = 32
DEAD = 255
EDGE = 48

cosine_eps = 1e-06
layer_eps = 1e-05
LOG2E = math.log2(math.e)
MIB = 1024 * 1024
LANES = 128

F32 = jnp.float32
BF16 = jnp.bfloat16


def divided(x, n):
    quotient = lax.div(x, jnp.full_like(x, n))
    return quotient, x - quotient * n


def window_parts(row):
    window, inner = divided(row, CELLS)
    level, inner = divided(inner, WA * WO)
    lat, lon = divided(inner, WO)
    return window, level, lat, lon


def dot(a, b):
    return jnp.dot(a, b, preferred_element_type=F32)


def selection(rows, columns):
    return (rows == columns).astype(F32).astype(BF16)


def pinned(x, space=pltpu.HBM):
    return pltpu.with_memory_space_constraint(x, space)


def pack_kernel(rows_ref, cells_ref, counts_ref, packed_ref):
    devices, capacity, channels = rows_ref.shape
    slots = devices * capacity
    for at in range(channels // LANES):
        part = rows_ref[:, :, at * LANES : (at + 1) * LANES]
        packed_ref[:, at * capacity : (at + 1) * capacity] = part
    cells = cells_ref[...]
    high = lax.div(cells, jnp.full_like(cells, DIGIT))
    low = cells - high * DIGIT
    slot = lax.broadcasted_iota(jnp.int32, (1, slots), 1)
    device = lax.broadcasted_iota(jnp.int32, (devices, 1), 0)
    place = lax.broadcasted_iota(jnp.int32, (slots, 1), 0)
    place = lax.rem(place, jnp.full_like(place, capacity))
    lane = lax.broadcasted_iota(jnp.int32, (1, LANES), 1)
    own = divided(slot, capacity)[0] == device
    digits = jnp.zeros((devices, LANES), F32)
    for i, digit in enumerate((high, low)):
        spread = jnp.where(own, digit.astype(F32), 0.0).astype(BF16)
        digits += dot(spread, selection(place + i * capacity, lane))
    same = device == lax.broadcasted_iota(jnp.int32, (1, devices), 1)
    count = jnp.sum(jnp.where(same, counts_ref[...].astype(F32), 0.0), -1, keepdims=True)
    dead = (lane < capacity) & (lane.astype(F32) >= count)
    digits = jnp.where(dead, float(DEAD), digits)
    packed_ref[:, channels // LANES * capacity :] = jnp.broadcast_to(
        digits[:, None, :], (devices, EXTRA, LANES)
    ).astype(BF16)


def pack(rows, cells, counts):
    devices, capacity, channels = rows.shape
    held = channels // LANES * capacity + EXTRA
    return pl.pallas_call(
        pack_kernel,
        out_shape=jax.ShapeDtypeStruct((devices, held, LANES), BF16),
        compiler_params=pltpu.CompilerParams(vmem_limit_bytes=16 * MIB),
    )(pinned(rows), pinned(cells), pinned(counts))


def project_kernel(
    lon_cells, latent_hbm, w_obs_hbm, w_hbm, bias_hbm, base_ref, folded_ref, scaled_ref, latent_ref,
    w_ref, left, sems,
):
    rows, features = latent_ref.shape
    part = WA * lon_cells
    strip = WL * part
    strips = rows // strip
    groups = features // GROUP
    windows = lon_cells // WO
    first, second = 8 * lon_cells, (WA - 8) * lon_cells

    def columns(j):
        at = lax.rem(j, 3) * groups + lax.div(j, 3)
        return pl.ds(pl.multiple_of(at * GROUP, GROUP), GROUP)

    def fetched(j):
        return pltpu.make_async_copy(w_hbm.at[:, columns(j)], w_ref.at[j], sems.at[j])

    copies = []
    for s in range(strips):
        for l in range(WL):
            lines = pl.ds((l * strips + s) * part, part)
            at = 3 * groups + len(copies)
            copies.append(
                pltpu.make_async_copy(latent_hbm.at[lines], latent_ref.at[lines], sems.at[at])
            )
    at = 3 * groups + len(copies)
    copies.append(pltpu.make_async_copy(w_obs_hbm, left.at[pl.ds(rows, w_obs_hbm.shape[0])], sems.at[at]))
    copies.append(pltpu.make_async_copy(bias_hbm, scaled_ref, sems.at[at + 1]))
    for copy in copies[:-1]:
        copy.start()
    for j in range(3 * groups):
        fetched(j).start()
    copies[-1].start()

    perms = []
    for lines in (first, second):
        run = lines // windows
        row = lax.broadcasted_iota(jnp.int32, (lines, 1), 0)
        window, inner = divided(row, run)
        lat, lon = divided(inner, WO)
        source = lat * lon_cells + window * WO + lon
        perms.append(selection(source, lax.broadcasted_iota(jnp.int32, (1, lines), 1)))
    for s in range(strips):
        moved = []
        for l in range(WL):
            copies[s * WL + l].wait()
            begin = (l * strips + s) * part
            moved.append(dot(perms[0], latent_ref[begin : begin + first]))
            moved.append(dot(perms[1], latent_ref[begin + first : begin + part]))
        for w in range(windows):
            runs = []
            for piece in moved:
                run = piece.shape[0] // windows
                runs.append(piece[w * run : (w + 1) * run])
            at = s * strip + w * CELLS
            left[at : at + CELLS] = jnp.concatenate(runs, axis=0).astype(BF16)
    copies[-2].wait()

    def multiply(j, carry):
        fetched(j).wait()
        result = dot(left[...], w_ref[j])
        base_ref[j] = result[:rows]
        folded_ref[j] = result[rows:].astype(BF16)
        return carry

    lax.fori_loop(0, 3 * groups, multiply, 0)
    copies[-1].wait()
    scaled_ref[...] = scaled_ref[...] * LOG2E


def project(latent, w_obs, w_qkv, bias, lon_cells):
    rows, features = latent.shape
    channels = w_obs.shape[0]
    columns = w_qkv.shape[1]
    blocks = columns // GROUP
    strips = rows // (WL * WA * lon_cells)
    there = pl.BlockSpec(memory_space=pl.ANY)
    here = pl.BlockSpec(memory_space=pltpu.VMEM)
    return pl.pallas_call(
        functools.partial(project_kernel, lon_cells),
        in_specs=[there] * 4,
        out_specs=[here] * 3,
        out_shape=[
            pltpu.VMEM((blocks, rows, GROUP), F32),
            pltpu.VMEM((blocks, channels, GROUP), BF16),
            pltpu.VMEM(bias.shape, F32),
        ],
        scratch_shapes=[
            pltpu.VMEM((rows, features), BF16),
            pltpu.VMEM((blocks, features, GROUP), BF16),
            pltpu.VMEM((rows + channels, features), BF16),
            pltpu.SemaphoreType.DMA((blocks + WL * strips + 2,)),
        ],
        compiler_params=pltpu.CompilerParams(vmem_limit_bytes=24 * MIB),
        cost_estimate=pl.CostEstimate(
            flops=2 * (rows + channels) * features * columns,
            bytes_accessed=4 * rows * columns + 2 * features * columns + 4 * rows * features,
            transcendentals=0,
        ),
    )(pinned(latent), pinned(w_obs), pinned(w_qkv), pinned(bias))


def in_output_order(target, at, window, block, lon_cells):
    for level in range(WL):
        for lat in range(WA):
            half, line = divmod(lat, HALF_A)
            row = (half * WL + (level + WL // 2) % WL) * HALF_A + line
            source = (level * WA + lat) * WO
            moved = window * WO + HALF_O
            begin = 0
            while begin < WO:
                goal = (moved + begin) % lon_cells
                count = min(WO - begin, lon_cells - goal)
                lines = slice(row * lon_cells + goal, row * lon_cells + goal + count)
                target[lines, at] = block[source + begin : source + begin + count]
                begin += count


def strip_kernel(
    strip_at,
    lon_cells,
    passed,
    packed_ref,
    scale_ref,
    gain_ref,
    base_ref,
    folded_ref,
    bias_ref,
    latent_hbm,
    w_obs_hbm,
    w_out_hbm,
    *rest,
):
    carried_ref = rest[0] if passed else None
    (
        near_ref,
        far_ref,
        edge_ref,
        latent_ref,
        w_obs_ref,
        w_out_ref,
        gathered,
        gathered_out,
        context,
        sems,
    ) = rest[passed:]
    lat_cells = latent_hbm.shape[1]
    features = w_out_ref.shape[0]
    strip = gathered.shape[0]
    windows = strip // CELLS
    groups = features // GROUP
    heads = bias_ref.shape[0] // groups
    width = GROUP // heads
    devices, held, _ = packed_ref.shape
    channels = w_obs_ref.shape[0]
    cuts = channels // LANES
    capacity = (held - EXTRA) // cuts
    copies = [
        pltpu.make_async_copy(
            latent_hbm.at[:, pl.ds(strip_at * WA, WA)], latent_ref, sems.at[0]
        ),
        pltpu.make_async_copy(w_obs_hbm, w_obs_ref, sems.at[1]),
        pltpu.make_async_copy(w_out_hbm, w_out_ref, sems.at[2]),
    ]

    for copy in copies:
        copy.start()
    row = lax.broadcasted_iota(jnp.int32, (strip, 1), 0)
    window, level, lat, lon = window_parts(row)
    cell = (level * lat_cells + strip_at * WA + lat) * lon_cells + window * WO + lon
    count = BLOCK * capacity
    slot = lax.broadcasted_iota(jnp.int32, (1, count), 1)
    source, place = divided(slot, capacity)
    lane = lax.broadcasted_iota(jnp.int32, (LANES, 1), 0)
    weigh = jnp.where(lane == place, float(DIGIT), 0.0) + jnp.where(
        lane == place + capacity, 1.0, 0.0
    )
    line = lax.broadcasted_iota(jnp.int32, (BLOCK * EXTRA, 1), 0)
    total = jnp.zeros((strip, channels), F32)
    for at in range(0, devices, BLOCK):
        some = slice(at, at + BLOCK)
        digits = packed_ref[some, cuts * capacity :].reshape(BLOCK * EXTRA, LANES)
        values = dot(digits, weigh.astype(BF16))
        target = jnp.sum(
            jnp.where(line == source * EXTRA, values, 0.0), 0, keepdims=True
        )
        rows = [
            packed_ref[some, c * capacity : (c + 1) * capacity].reshape(count, LANES)
            for c in range(cuts)
        ]
        rows = jnp.concatenate(rows, axis=1)
        total += dot(selection(cell, target.astype(jnp.int32)), rows)
    gathered[...] = total.astype(BF16)
    for w in range(windows):
        block = total[w * CELLS : (w + 1) * CELLS]
        in_output_order(gathered_out, slice(None), w, block, lon_cells)

    lane_head = lax.broadcasted_iota(jnp.int32, (1, GROUP), 1) // width
    same_head = selection(lax.broadcasted_iota(jnp.int32, (GROUP, 1), 0) // width, lane_head)
    left_half = lax.broadcasted_iota(jnp.int32, (CELLS, 2 * width), 1) < width
    blank = jnp.zeros((width, CELLS), BF16)

    mine = slice(strip_at * strip, (strip_at + 1) * strip)

    def group(step, carry):
        scale = jnp.zeros((1, GROUP), F32)
        for h in range(heads):
            scale = jnp.where(lane_head == h, scale_ref[step * heads + h] * LOG2E, scale)
        high = gathered[...]
        query, keys, values = (
                base_ref[3 * step + i, mine] + dot(high, folded_ref[3 * step + i]) for i in range(3)
            )
        query_sum = dot((query * query).astype(BF16), same_head)
        query_n = (query * (lax.rsqrt(query_sum + cosine_eps) * scale)).astype(BF16)

        def scored(w):
            here = slice(w * CELLS, (w + 1) * CELLS)
            keys_t = keys[here].T
            result = []
            for h in range(heads):
                pair, side = h // 2, h % 2
                lanes = slice(2 * pair * width, 2 * (pair + 1) * width)
                own = keys_t[h * width : (h + 1) * width]
                own = own * lax.rsqrt(jnp.sum(own * own, 0, keepdims=True) + cosine_eps)
                own = own.astype(BF16)
                own = jnp.concatenate([blank, own] if side else [own, blank], axis=0)
                result.append(dot(query_n[here, lanes], own))
            return result

        def weighted(w, scores):
            here = slice(w * CELLS, (w + 1) * CELLS)
            expo = [jnp.exp2(scores[h] + bias_ref[step * heads + h]).astype(BF16) for h in range(heads)]
            sums = []
            for h in range(heads):
                lanes = slice(h // 2 * 2 * width, (h // 2 + 1) * 2 * width)
                mixed = jnp.where(left_half == (h % 2 == 0), values[here, lanes], 1.0).astype(BF16)
                sums.append(dot(expo[h], mixed))
            parts = []
            for a, b in zip(sums[::2], sums[1::2]):
                norm = pltpu.roll(jnp.where(left_half, b, a), width, 1)
                guess = pl.reciprocal(norm, approx=True)
                parts.append(jnp.where(left_half, a, b) * (guess * (2.0 - norm * guess)))
            in_output_order(
                context.at[step], slice(None), w, jnp.concatenate(parts, axis=1), lon_cells
            )

        scores = scored(0)
        for w in range(windows):
            after = scored(w + 1) if w + 1 < windows else None
            weighted(w, scores)
            scores = after
        return carry

    lax.fori_loop(0, groups, group, 0)

    for copy in copies:
        copy.wait()
    size = strip // 2
    line, moved = divided(lax.broadcasted_iota(jnp.int32, (1, size), 1), lon_cells)
    wanted = jnp.where(moved < HALF_O, line * HALF_O + moved, -1)
    pick = selection(lax.broadcasted_iota(jnp.int32, (EDGE, 1), 0), wanted)
    halves = [slice(h * size, (h + 1) * size) for h in range(2)]
    projs = [
        dot(
            jnp.concatenate([context[g, here].astype(BF16) for g in range(groups)], axis=1),
            w_out_ref[...],
        )
        for here in halves
    ]
    added = [dot(gathered_out[here].astype(BF16), w_obs_ref[...]) for here in halves]
    for h, out_ref in enumerate((near_ref, far_ref)):
        runs = []
        for l in range(WL):
            own = latent_ref[(l - WL // 2) % WL, h * HALF_A : (h + 1) * HALF_A].astype(F32)
            own = jnp.concatenate(
                [own[:, lon_cells - HALF_O :], own[:, : lon_cells - HALF_O]], axis=1
            )
            runs.append(own.reshape(HALF_A * lon_cells, features))
        latent = jnp.concatenate(runs, axis=0) + added[h]
        proj = projs[h]
        center = proj - jnp.mean(proj, -1, keepdims=True)
        spread = jnp.mean(center * center, -1, keepdims=True)
        normed = center * lax.rsqrt(spread + layer_eps) * gain_ref[...]
        done = (latent + normed).astype(BF16)
        out_ref[...] = done
        if h == 0 or passed:
            edge_ref[h * EDGE : (h + 1) * EDGE] = dot(pick, done).astype(BF16)
    if passed:
        edge_ref[2 * EDGE :] = carried_ref[...]


def attend_strip(
    strip_at, packed, scale, gain, base, folded, bias, latent, w_obs, w_out, carried=None
):
    levels, lat_cells, lon_cells, features = latent.shape
    strip = WL * WA * lon_cells
    groups = features // GROUP
    channels = w_obs.shape[0]
    heads = bias.shape[0] // groups
    passed = carried is not None
    there = pl.BlockSpec(memory_space=pl.ANY)
    here = pl.BlockSpec(memory_space=pltpu.VMEM)
    half = (strip // 2, features)
    outs = [half, half, (3 * EDGE if passed else EDGE, features)]
    extra = [carried] if passed else []
    return pl.pallas_call(
        functools.partial(strip_kernel, strip_at, lon_cells, passed),
        in_specs=[here, pl.BlockSpec(memory_space=pltpu.SMEM)]
        + [here] * 4
        + [there] * 3
        + [here] * len(extra),
        out_specs=[here] * 3,
        out_shape=[jax.ShapeDtypeStruct(shape, BF16) for shape in outs],
        scratch_shapes=[
            pltpu.VMEM((levels, WA, lon_cells, features), BF16),
            pltpu.VMEM(w_obs.shape, BF16),
            pltpu.VMEM(w_out.shape, BF16),
            pltpu.VMEM((strip, channels), BF16),
            pltpu.VMEM((strip, channels), F32),
            pltpu.VMEM((groups, strip, GROUP), F32),
            pltpu.SemaphoreType.DMA((3,)),
        ],
        compiler_params=pltpu.CompilerParams(vmem_limit_bytes=24 * MIB),
        cost_estimate=pl.CostEstimate(
            flops=14 * strip * features * features,
            bytes_accessed=12 * strip * features + 8 * features * features,
            transcendentals=strip * CELLS * bias.shape[0],
        ),
    )(
        packed,
        scale,
        gain,
        pinned(base, pltpu.VMEM),
        pinned(folded, pltpu.VMEM),
        pinned(bias, pltpu.VMEM),
        pinned(latent),
        pinned(w_obs),
        pinned(w_out),
        *extra,
    )


def corner_kernel(lon_cells, block_ref, edge_ref):
    size = block_ref.shape[0]
    line, moved = divided(lax.broadcasted_iota(jnp.int32, (1, size), 1), lon_cells)
    wanted = jnp.where(moved < HALF_O, line * HALF_O + moved, -1)
    index = lax.broadcasted_iota(jnp.int32, (EDGE, 1), 0)
    edge_ref[...] = dot(selection(index, wanted), block_ref[...]).astype(BF16)


def corner(block, lon_cells):
    size, features = block.shape
    return pl.pallas_call(
        functools.partial(corner_kernel, lon_cells),
        out_shape=jax.ShapeDtypeStruct((EDGE, features), BF16),
        compiler_params=pltpu.CompilerParams(vmem_limit_bytes=16 * MIB),
        cost_estimate=pl.CostEstimate(
            flops=2 * EDGE * size * features, bytes_accessed=2 * size * features, transcendentals=0
        ),
    )(block)


def join_kernel(lon_cells, count, *refs):
    ins, (out_hbm, blocks, sems) = refs[:-3], refs[-3:]
    size = WL * HALF_A * lon_cells
    half = size // WL
    row = lax.broadcasted_iota(jnp.int32, (size, 1), 0)
    line, moved = divided(row, lon_cells)
    edge = jnp.where(moved < HALF_O, line * HALF_O + moved, -1)
    insert = selection(edge, lax.broadcasted_iota(jnp.int32, (1, EDGE), 1))
    copies = []
    for at in range(count):
        block_ref, edge_ref, edge_at = ins[2 * at], ins[2 * at + 1], (0, 0, 1, 2)[at]
        west = dot(insert, edge_ref[edge_at * EDGE : (edge_at + 1) * EDGE])
        full = jnp.where(moved < HALF_O, west, block_ref[...].astype(F32)).astype(BF16)
        for l in range(WL):
            blocks[at, l] = full[l * half : (l + 1) * half]
        copies.append(pltpu.make_async_copy(blocks.at[at], out_hbm.at[:, at], sems.at[at]))
        copies[-1].start()
    for copy in copies:
        copy.wait()


def join(blocks, lon_cells):
    features = blocks[0][0].shape[-1]
    size = WL * HALF_A * lon_cells
    flat = [part for block in blocks for part in block]
    return pl.pallas_call(
        functools.partial(join_kernel, lon_cells, len(blocks)),
        in_specs=[pl.BlockSpec(memory_space=pltpu.VMEM)] * len(flat),
        out_specs=pl.BlockSpec(memory_space=pl.ANY),
        out_shape=jax.ShapeDtypeStruct((WL, len(blocks), size // WL, features), BF16),
        scratch_shapes=[
            pltpu.VMEM((len(blocks), WL, size // WL, features), BF16),
            pltpu.SemaphoreType.DMA((len(blocks),)),
        ],
        compiler_params=pltpu.CompilerParams(vmem_limit_bytes=16 * MIB),
        cost_estimate=pl.CostEstimate(
            flops=0, bytes_accessed=4 * len(blocks) * size * features, transcendentals=0
        ),
    )(*flat)


def body(
    latent_state,
    obs_rows,
    obs_cells,
    obs_counts,
    w_obs,
    w_qkv,
    w_out,
    logit_scale,
    pos_bias,
    out_gain,
):
    levels, lat_cells, lon_cells, features = latent_state.shape
    lat_devices = lax.axis_size("lat")
    lon_devices = lax.axis_size("lon")
    devices = lat_devices * lon_devices
    both = ("lat", "lon")
    capacity = obs_rows.shape[2] // devices
    channels = obs_rows.shape[3]

    packed = pack(
        obs_rows.reshape(devices, capacity, channels),
        obs_cells.reshape(1, devices * capacity),
        obs_counts.reshape(1, devices),
    )
    packed = lax.all_to_all(packed, both, split_axis=0, concat_axis=0, tiled=True)
    base, folded, bias = project(
        latent_state.reshape(-1, features), w_obs, w_qkv, pos_bias, lon_cells
    )
    gain = out_gain[None]

    def attend(strip_at, carried=None):
        return attend_strip(
            strip_at, packed, logit_scale, gain, base, folded, bias, latent_state, w_obs, w_out, carried
        )

    south = [(i, i + 1) for i in range(lat_devices - 1)]
    east = [(i, (i + 1) % lon_devices) for i in range(lon_devices)]
    low_near, low_far, low_edge = attend(1)
    first = lax.ppermute(low_far, "lat", south)
    top_near, top_far, edges = attend(0, low_edge)
    edges = lax.ppermute(edges, "lon", east)
    first_edge = lax.ppermute(corner(first, lon_cells), "lon", east)
    joined = join(
        [
            (first, first_edge),
            (top_near, edges),
            (top_far, edges),
            (low_near, edges),
        ],
        lon_cells,
    )
    return joined.reshape(levels, lat_cells, lon_cells, features)


def solution(mesh):
    in_specs = (
        P(None, "lat", "lon", None),
        P("lat", "lon", None, None),
        P("lat", "lon", None),
        P("lat", "lon", None),
        P(),
        P(),
        P(),
        P(),
        P(),
        P(),
    )
    out_specs = P(None, "lat", "lon", None)
    return jax.shard_map(body, mesh=mesh, in_specs=in_specs, out_specs=out_specs, check_vma=False)
```
